32 devices in a mesh: wide: 8 (over z, y), narrow: 4 (over x, core).
Axes of the slice: x: 2, y: 2, z: 4, core: 2. Of those that a mesh axis runs over, the one named last changes fastest.
Arguments:
- text_tokens: bfloat16 [256, 256, 512], P(('wide', 'narrow')), may hold values from -6 to 6
- memory: bfloat16 [256, 256, 512], P(('wide', 'narrow')), may hold values from -6 to 6
- cotangent: bfloat16 [256, 256, 512], P(('wide', 'narrow')), may hold values from -6 to 6
- lengths: int32 [256], P(('wide', 'narrow')), may hold values from 1 to 256, as said below
- memory_mask: int32 [256, 256], P(('wide', 'narrow')), may hold values from 0 to 1, as said below
- group_table: int32 [8], replicated, may hold values from 0 to 1, as said below
- self_gain: float32 [512], replicated, may hold values from 0.5 to 1.5
- cross_gain: float32 [512], replicated, may hold values from 0.5 to 1.5
- ffn_gain: float32 [512], replicated, may hold values from 0.5 to 1.5
- self_query: bfloat16 [512, 384], replicated, may hold values from -0.25 to 0.25
- self_key: bfloat16 [512, 384], replicated, may hold values from -0.25 to 0.25
- self_value: bfloat16 [512, 384], replicated, may hold values from -0.25 to 0.25
- self_out: bfloat16 [384, 512], replicated, may hold values from -1.25 to 1.25
- cross_query: bfloat16 [512, 384], replicated, may hold values from -0.25 to 0.25
- cross_key: bfloat16 [512, 384], replicated, may hold values from -0.25 to 0.25
- cross_value: bfloat16 [512, 384], replicated, may hold values from -0.25 to 0.25
- cross_out: bfloat16 [384, 512], replicated, may hold values from -1.25 to 1.25
- ffn_gate: bfloat16 [512, 1024], replicated, may hold values from -0.25 to 0.25
- ffn_up: bfloat16 [512, 1024], replicated, may hold values from -0.25 to 0.25
- ffn_down: bfloat16 [1024, 512], replicated, may hold values from -0.1875 to 0.1875
Outputs:
- layer_output: bfloat16 [256, 256, 512], P(('wide', 'narrow'))
- text_grad: bfloat16 [256, 256, 512], P(('wide', 'narrow'))
- memory_grad: bfloat16 [256, 256, 512], P(('wide', 'narrow'))
- self_gain_grad: float32 [512], replicated
- cross_gain_grad: float32 [512], replicated
- ffn_gain_grad: float32 [512], replicated
- self_query_grad: float32 [512, 384], replicated
- self_key_grad: float32 [512, 384], replicated
- self_value_grad: float32 [512, 384], replicated
- self_out_grad: float32 [384, 512], replicated
- cross_query_grad: float32 [512, 384], replicated
- cross_key_grad: float32 [512, 384], replicated
- cross_value_grad: float32 [512, 384], replicated
- cross_out_grad: float32 [384, 512], replicated
- ffn_gate_grad: float32 [512, 1024], replicated
- ffn_up_grad: float32 [512, 1024], replicated
- ffn_down_grad: float32 [1024, 512], replicated
- group_counts: float32 [2], replicated
The draws below stay inside these ranges and needn't reach their ends.
Inputs may be any that keep to these rules, and one draw needn't show every extreme that they name: `lengths`: number of leading valid text slots of each item. `memory_mask`: every item has at least one valid memory token. `group_table`: each of the 2 groups holds at least one wide position.
All inputs are finite; a program needn't handle non-finite values.
Results may differ from the reference program's by a relative error of at most 0.02.
The reference program's roundings to bfloat16 on the way (of `self_input`) count: a program that leaves them out, or rounds other values in their place, can miss the bound.
Values sent between devices are 32-bit elements; how exact they have to be, the bound alone decides.
A program may use at most 256 MiB of HBM per device.

```python
import jax
import jax.numpy as jnp
from jax import lax

D = 512
HEADS = 6
HEAD = 64
FF = 1024
S = 256
M = 256
GROUPS = 2
ITEMS_DEV = 8
INNER = 384
ITEMS = 256
N_WIDE = 8
N_NARROW = 4


def draw_lengths(key, part):
    key = jax.random.fold_in(key, 11)
    index = jnp.arange(ITEMS, dtype=jnp.int32)
    ceiling = S // 3 + (S - S // 3) * index // max(ITEMS - 1, 1)
    return jax.random.randint(key, (ITEMS,), 1, ceiling + 1, dtype=jnp.int32)


def draw_memory_mask(key, part):
    key = jax.random.fold_in(key, 23)
    first_key, second_key = jax.random.split(key)
    coins = jax.random.randint(first_key, (ITEMS, M), 0, 4, dtype=jnp.int32)
    chosen = jax.random.randint(second_key, (ITEMS, 1), 0, M, dtype=jnp.int32)
    positions = jnp.arange(M, dtype=jnp.int32)[None, :]
    return jnp.where((coins > 0) | (positions == chosen), 1, 0).astype(jnp.int32)


def draw_group_table(key, part):
    key = jax.random.fold_in(key, 37)
    first_key, second_key = jax.random.split(key)
    robots = jax.random.randint(first_key, (), 1, N_WIDE, dtype=jnp.int32)
    ordering = jax.random.permutation(second_key, N_WIDE).astype(jnp.int32)
    return (ordering < robots).astype(jnp.int32)


def shard_levels(key, extent, shards, smallest, largest):
    def one(position, blocks):
        steps = jax.random.uniform(jax.random.fold_in(jax.random.fold_in(key, 6), position), (blocks,), jnp.float32, smallest / len(shards), largest / len(shards))
        return jnp.repeat(jnp.exp(steps), extent[position] // blocks).reshape((-1,) + (1,) * (len(extent) - position - 1))

    level = one(*shards[0])
    for cut in shards[1:]:
        level = level * one(*cut)
    return level


def gaussian(stream_key, extent, scale, reach, shards=(), kind=jnp.bfloat16):
    level = shard_levels(stream_key, extent, shards, -0.22, 0.18) if shards else 1.0
    values = jax.random.normal(stream_key, extent, jnp.float32) * scale * level
    return jnp.minimum(jnp.maximum(values, -reach), reach).astype(kind)


def setup_inputs(seed: int = 0) -> dict:
    keys = jax.random.split(jax.random.key(seed), 21)
    return {
        "text_tokens": gaussian(keys[0], (ITEMS, S, D), 1.0, 6.0, ((0, 32),)),
        "memory": gaussian(keys[1], (ITEMS, M, D), 1.0, 6.0, ((0, 32),)),
        "cotangent": gaussian(keys[2], (ITEMS, S, D), 1.0, 6.0, ((0, 32),)),
        "lengths": draw_lengths(jax.random.fold_in(keys[20], 71), 0),
        "memory_mask": draw_memory_mask(jax.random.fold_in(keys[20], 71), 0),
        "group_table": draw_group_table(jax.random.fold_in(keys[20], 71), 0),
        "self_gain": jnp.clip(1.0 + 0.1 * jax.random.normal(keys[6], (D,), jnp.float32), 0.5, 1.5),
        "cross_gain": jnp.clip(1.0 + 0.1 * jax.random.normal(keys[7], (D,), jnp.float32), 0.5, 1.5),
        "ffn_gain": jnp.clip(1.0 + 0.1 * jax.random.normal(keys[8], (D,), jnp.float32), 0.5, 1.5),
        "self_query": gaussian(keys[9], (D, INNER), D ** -0.5, 0.25),
        "self_key": gaussian(keys[10], (D, INNER), D ** -0.5, 0.25),
        "self_value": gaussian(keys[11], (D, INNER), D ** -0.5, 0.25),
        "self_out": gaussian(keys[12], (INNER, D), (INNER // 16) ** -0.5, 1.25),
        "cross_query": gaussian(keys[13], (D, INNER), D ** -0.5, 0.25),
        "cross_key": gaussian(keys[14], (D, INNER), D ** -0.5, 0.25),
        "cross_value": gaussian(keys[15], (D, INNER), D ** -0.5, 0.25),
        "cross_out": gaussian(keys[16], (INNER, D), (INNER // 16) ** -0.5, 1.25),
        "ffn_gate": gaussian(keys[17], (D, FF), D ** -0.5, 0.25),
        "ffn_up": gaussian(keys[18], (D, FF), D ** -0.5, 0.25),
        "ffn_down": gaussian(keys[19], (FF, D), FF ** -0.5, 0.1875),
    }


EPSILON = 1e-06
PRECISE = lax.Precision.HIGHEST

@jax.custom_vjp
def low(v):
    return lax.optimization_barrier(v.astype(jnp.bfloat16)).astype(jnp.float32)

@jax.custom_vjp
def low_back(v):
    return v

def low_keep(v):
    return (low(v), None)

def low_pass(kept, grad):
    return (grad,)

def back_keep(v):
    return (v, None)

def back_low(kept, grad):
    return (low(grad),)
low.defvjp(low_keep, low_pass)
low_back.defvjp(back_keep, back_low)

def rms_norm(values, gain):
    return values * lax.rsqrt(lax.optimization_barrier(jnp.mean(values * values, axis=-1, keepdims=True)) + EPSILON) * gain

def project(inputs, weight):
    return jnp.einsum('isd,de->ise', inputs, weight, precision=PRECISE)

def attend(query_in, key_in, w_query, w_key, w_value, w_out, allowed):
    item_count = query_in.shape[0]
    row_count = query_in.shape[1]
    key_count = key_in.shape[1]
    query_heads = low_back(low(project(query_in, w_query))).reshape(item_count, row_count, HEADS, HEAD)
    key_heads = low_back(low(project(key_in, w_key))).reshape(item_count, key_count, HEADS, HEAD)
    value_heads = low_back(low(project(key_in, w_value))).reshape(item_count, key_count, HEADS, HEAD)
    scores = low_back(jnp.einsum('iqhe,ikhe->ihqk', query_heads, key_heads, precision=PRECISE) * HEAD ** (-0.5))
    scores = jnp.where(allowed[:, None], scores, -1e+30)
    probabilities = low(jax.nn.softmax(scores, axis=-1))
    mixture = jnp.einsum('ihqk,ikhe->iqhe', probabilities, value_heads, precision=PRECISE)
    mixture = low_back(low(mixture.reshape(item_count, row_count, HEADS * HEAD)))
    return low_back(project(mixture, w_out))

def layer(text_in, memory_in, params, self_allowed, cross_allowed):
    self_gain, cross_gain, ffn_gain, s_query, s_key, s_value, s_out, c_query, c_key, c_value, c_out, w_gate, w_up, w_down = params
    self_input = low(rms_norm(text_in, self_gain))
    after_self = text_in + attend(self_input, self_input, s_query, s_key, s_value, s_out, self_allowed)
    cross_input = low(rms_norm(after_self, cross_gain))
    after_cross = after_self + attend(cross_input, memory_in, c_query, c_key, c_value, c_out, cross_allowed)
    ffn_input = low(rms_norm(after_cross, ffn_gain))
    gate_proj = low_back(project(ffn_input, w_gate))
    up_proj = low_back(project(ffn_input, w_up))
    active = low(jax.nn.gelu(gate_proj, approximate=True) * up_proj)
    return after_cross + low_back(project(active, w_down))

def reference(text_tokens, memory, cotangent, lengths, memory_mask, group_table, self_gain, cross_gain, ffn_gain, self_query, self_key, self_value, self_out, cross_query, cross_key, cross_value, cross_out, ffn_gate, ffn_up, ffn_down):
    devices = N_WIDE * N_NARROW
    positions = jnp.arange(S, dtype=jnp.int32)
    valid_mask = (positions[None, :] < lengths[:, None]).astype(jnp.float32)
    item_place = jnp.arange(ITEMS, dtype=jnp.int32) // (ITEMS_DEV * N_NARROW)
    item_group = group_table[item_place]
    group_ids = jnp.arange(GROUPS, dtype=jnp.int32)
    one_hot = (item_group[:, None] == group_ids[None, :]).astype(jnp.float32)
    counts = lax.optimization_barrier(jnp.sum(one_hot * lax.optimization_barrier(jnp.sum(valid_mask, axis=1))[:, None], axis=0))
    root_counts = jnp.sqrt(counts)
    factors = jnp.sum(counts) / (jnp.sum(root_counts) * root_counts)
    owners = group_table[jnp.arange(devices, dtype=jnp.int32) // N_NARROW]
    device_factor = lax.optimization_barrier(jnp.sum(jnp.where(owners[:, None] == group_ids[None, :], factors[None, :], 0.0), axis=1))
    params = tuple((entry.astype(jnp.float32) for entry in (self_gain, cross_gain, ffn_gain, self_query, self_key, self_value, self_out, cross_query, cross_key, cross_value, cross_out, ffn_gate, ffn_up, ffn_down)))

    def by_device(array):
        return array.reshape((devices, ITEMS_DEV) + array.shape[1:])

    def block_step(carry, inputs):
        text_block, memory_block, cot_block, length_block, mask_block, valid_block, factor_block = inputs
        self_allowed = (positions[None, :, None] >= positions[None, None, :]) & (positions[None, None, :] < length_block[:, None, None])
        cross_allowed = (mask_block > 0)[:, None, :]

        def forward(text_in, memory_in, weights):
            return layer(text_in, memory_in, weights, self_allowed, cross_allowed)
        result, pullback = jax.vjp(forward, text_block.astype(jnp.float32), memory_block.astype(jnp.float32), params)
        text_back, memory_back, param_back = pullback(cot_block.astype(jnp.float32) * valid_block[:, :, None])
        carry = tuple((total + factor_block * entry for total, entry in zip(carry, param_back)))
        return (carry, (result.astype(jnp.bfloat16), (factor_block * text_back).astype(jnp.bfloat16), (factor_block * memory_back).astype(jnp.bfloat16)))
    zero_grads = tuple((jnp.zeros(entry.shape, jnp.float32) for entry in params))
    totals, stacked = lax.scan(block_step, zero_grads, (by_device(text_tokens), by_device(memory), by_device(cotangent), by_device(lengths), by_device(memory_mask), by_device(valid_mask), device_factor))
    layer_output = stacked[0].reshape(ITEMS, S, D)
    text_grad = stacked[1].reshape(ITEMS, S, D)
    memory_grad = stacked[2].reshape(ITEMS, M, D)
    return (layer_output, text_grad, memory_grad, totals[0], totals[1], totals[2], totals[3], totals[4], totals[5], totals[6], totals[7], totals[8], totals[9], totals[10], totals[11], totals[12], totals[13], counts)
```

```python
import functools

import jax
import jax.numpy as jnp
from jax import lax
from jax.experimental import pallas as pl
from jax.experimental.pallas import tpu as pltpu
from jax.sharding import PartitionSpec as P

HEADS = 6
GROUPS = 2
EPSILON = 1e-06
NEGATIVE = -1e30
F32 = jnp.float32
BF16 = jnp.bfloat16
AXES = ("wide", "narrow")
ROOT = 0.7978845608028654
CUBE = 0.044715
MIB = 1 << 20


def contract(left, right, left_dim, right_dim):
    return lax.dot_general(
        left, right, (((left_dim,), (right_dim,)), ((), ())), preferred_element_type=F32
    )


def nn(left, right):
    return contract(left, right, 1, 0)


def nt(left, right):
    return contract(left, right, 1, 1)


def tn(left, right):
    return contract(left, right, 0, 0)


def norm_scale(values):
    return lax.rsqrt(jnp.mean(values * values, axis=-1, keepdims=True) + EPSILON)


def norm_back(values, gain, grad):
    scale = norm_scale(values)
    unit = values * scale
    gain_rows = grad * unit
    dot = jnp.mean(gain_rows * gain, axis=-1, keepdims=True)
    return scale * (grad * gain - unit * dot), jnp.sum(gain_rows, axis=0, keepdims=True)


def low_lanes(rows):
    return lax.broadcasted_iota(jnp.int32, (rows, 128), 1) < 64


def stack_heads(pair, low):
    zero = jnp.zeros_like(pair)
    return jnp.concatenate([jnp.where(low, pair, zero), jnp.where(low, zero, pair)], axis=0)


def pick_heads(stacked, low):
    rows = stacked.shape[0] // 2
    return jnp.where(low, stacked[:rows], stacked[rows:])


def pair_slice(values, index):
    return values[:, 128 * index : 128 * index + 128]


def attend(query, key, value, mask, qkv_ref, prob_ref, mix_ref):
    rows = query.shape[0]
    low = low_lanes(rows)
    query = (query * 0.125).astype(BF16)
    key = key.astype(BF16)
    value = value.astype(BF16)
    mixed = []
    for j in range(HEADS // 2):
        q, k, v = pair_slice(query, j), pair_slice(key, j), pair_slice(value, j)
        qkv_ref[j, 0, :, 0:128] = q
        qkv_ref[j, 0, :, 128:256] = k
        qkv_ref[j, 0, :, 256:384] = v
        scores = mask(nt(stack_heads(q, low), k))
        top = jnp.max(scores, axis=-1, keepdims=True)
        expo = jnp.exp(scores - top)
        total = jnp.sum(expo, axis=-1, keepdims=True)
        prob = (expo * (1.0 / total)).astype(BF16)
        prob_ref[j, 0] = prob
        mixed.append(pick_heads(nn(prob, v), low))
    mixture = jnp.concatenate(mixed, axis=1).astype(BF16)
    mix_ref[0] = mixture
    return mixture


def forward_kernel(
    len_ref, text_ref, mem_ref, mask_ref, self_gain, cross_gain, ffn_gain,
    sq_ref, sk_ref, sv_ref, so_ref, cq_ref, ck_ref, cv_ref, co_ref,
    sqkv_ref, sprob_ref, smix_ref, mid_ref, cin_ref, cqkv_ref, cprob_ref, cmix_ref, post_ref, fin_ref,
    wqkv, wkv,
):
    item = pl.program_id(0)
    inner = sq_ref.shape[1]

    @pl.when(item == 0)
    def _():
        wqkv[:, :inner] = sq_ref[...]
        wqkv[:, inner : 2 * inner] = sk_ref[...]
        wqkv[:, 2 * inner :] = sv_ref[...]
        wkv[:, :inner] = ck_ref[...]
        wkv[:, inner:] = cv_ref[...]

    rows = text_ref.shape[1]
    length = len_ref[item]
    row = lax.broadcasted_iota(jnp.int32, (2 * rows, rows), 0)
    row = jnp.where(row >= rows, row - rows, row)
    col = lax.broadcasted_iota(jnp.int32, (2 * rows, rows), 1)
    allowed = (col <= row) & (col < length)
    text = text_ref[0].astype(F32)
    self_in = (text * norm_scale(text) * self_gain[...]).astype(BF16)
    proj = nn(self_in, wqkv[...])
    mixture = attend(
        proj[:, :inner], proj[:, inner : 2 * inner], proj[:, 2 * inner :],
        lambda s: jnp.where(allowed, s, NEGATIVE), sqkv_ref, sprob_ref, smix_ref,
    )
    mid = text + nn(mixture, so_ref[...])
    mid_ref[0] = mid
    cross_in = (mid * norm_scale(mid) * cross_gain[...]).astype(BF16)
    cin_ref[0] = cross_in
    query = nn(cross_in, cq_ref[...])
    proj = nn(mem_ref[0], wkv[...])
    open_keys = mask_ref[pl.ds(item, 1), :] > 0
    mixture = attend(
        query, proj[:, :inner], proj[:, inner:],
        lambda s: jnp.where(open_keys, s, NEGATIVE), cqkv_ref, cprob_ref, cmix_ref,
    )
    post = mid + nn(mixture, co_ref[...])
    post_ref[0] = post
    fin_ref[0] = (post * norm_scale(post) * ffn_gain[...]).astype(BF16)


def forward(lengths, text, memory, mask, gains, weights):
    items, rows, width = text.shape
    inner = weights[0].shape[1]
    pairs = HEADS // 2

    def whole(array):
        zeros = (0,) * array.ndim
        return pl.BlockSpec(array.shape, lambda i: zeros)

    def per_item(*shape):
        zeros = (0,) * len(shape)
        return pl.BlockSpec((1,) + shape, lambda i: (i,) + zeros)

    def per_pair(*shape):
        return pl.BlockSpec((pairs, 1) + shape, lambda i: (0, i, 0, 0))

    qkv_shape = jax.ShapeDtypeStruct((pairs, items, rows, 384), BF16)
    prob_shape = jax.ShapeDtypeStruct((pairs, items, 2 * rows, rows), BF16)
    mix_shape = jax.ShapeDtypeStruct((items, rows, inner), BF16)
    full_shape = jax.ShapeDtypeStruct((items, rows, width), F32)
    half_shape = jax.ShapeDtypeStruct((items, rows, width), BF16)
    qkv_spec, prob_spec = per_pair(rows, 384), per_pair(2 * rows, rows)
    mix_spec, row_spec = per_item(rows, inner), per_item(rows, width)
    return pl.pallas_call(
        forward_kernel,
        grid=(items,),
        in_specs=[pl.BlockSpec(memory_space=pltpu.SMEM), row_spec, row_spec, whole(mask)]
        + [whole(g) for g in gains]
        + [whole(w) for w in weights],
        out_specs=[qkv_spec, prob_spec, mix_spec, row_spec, row_spec, qkv_spec, prob_spec, mix_spec, row_spec, row_spec],
        out_shape=[qkv_shape, prob_shape, mix_shape, full_shape, half_shape, qkv_shape, prob_shape, mix_shape, full_shape, half_shape],
        scratch_shapes=[pltpu.VMEM((width, 3 * inner), BF16), pltpu.VMEM((width, 2 * inner), BF16)],
        compiler_params=pltpu.CompilerParams(vmem_limit_bytes=63 * MIB),
        name="forward",
    )(lengths, text, memory, mask, *gains, *weights)


RISE = (0, 1, 3, 5, 6, 8, 9, 11, 13, 15)
HALVES = 5
LEGS = 2 * HALVES - 1


def exchange_plan():
    wide, narrow = lax.axis_index("wide"), lax.axis_index("narrow")
    z, y = wide // 2, wide % 2
    x, core = narrow // 2, narrow % 2
    near, far = z % 2, z // 2
    flip_x = (wide, (1 - x) * 2 + core)
    flip_y = (z * 2 + 1 - y, narrow)
    flip_core = (wide, x * 2 + 1 - core)
    flip_near = ((far * 2 + 1 - near) * 2 + y, narrow)
    flip_far = (((1 - far) * 2 + near) * 2 + y, narrow)

    def choose(first, second):
        return first + core * (second - first)

    first_flip = tuple(choose(a, b) for a, b in zip(flip_x, flip_y))
    third_flip = tuple(choose(b, a) for a, b in zip(flip_x, flip_y))
    bits = (core, choose(x, y), near, choose(y, x), far)
    partners = (flip_core, first_flip, flip_near, third_flip, flip_far)
    plain = (flip_core, flip_x, flip_near, flip_y, flip_far)
    return bits, partners, plain


def backward_kernel(
    linked, items, rows, width, inner, hidden,
    len_ref, group_ref, self_gain, cross_gain, ffn_gain,
    fin_hbm, cot_hbm, gate_hbm, up_hbm, down_hbm, post_hbm,
    cqkv_hbm, cprob_hbm, cmix_hbm, cq_hbm, ck_hbm, cv_hbm, co_hbm, cin_hbm, mem_hbm, mid_hbm,
    sqkv_hbm, sprob_hbm, smix_hbm, sq_hbm, sk_hbm, sv_hbm, so_hbm, text_hbm,
    out_hbm, text_grad_hbm, mem_grad_hbm, *rest,
):
    if linked:
        outs, rest = rest[:11], rest[11:]
        gain_grads, counts_ref, grads = rest[0], rest[1], rest[2]
        halves, small, small_in, factor_ref, send_sem, recv_sem, small_send, small_recv, done_sem, free_sem = rest[3:13]
        rest = rest[13:]
    else:
        grads, gain_grads = rest[:2]
        rest = rest[2:]
    (xf, din, first, second, first_t, second_t, gate, up, down, work,
    wqkv, wout, qkv, prob, mix, dmix, stage, load_sem, out_sem) = rest
    pairs = HEADS // 2
    chunk = 256
    chunks = hidden // chunk
    low = low_lanes(rows)
    units = 2 * chunks + 2 * (1 + pairs)
    last_tick = 2 * (units - 1) + RISE[-1]
    if linked:
        bits, partners, plain = exchange_plan()
        barrier = pltpu.get_barrier_semaphore()
        for device in (plain[0], plain[1], plain[2], plain[3], plain[4]):
            pl.semaphore_signal(barrier, inc=1, device_id=device, device_id_type=pl.DeviceIdType.MESH)
        pl.semaphore_wait(barrier, len(plain))

    half = 3 * width // 2

    def region(step, own):
        start = 0
        for s in range(step + 1):
            bit = bits[s] if own or s < step else 1 - bits[s]
            start = start + bit * (half >> s)
        return pl.ds(pl.multiple_of(start, 16), half >> step)

    def half_rows(step):
        size = half >> min(step, HALVES - 2)
        return pl.ds(2 * half - (2 * half >> step), size)

    def stage_copy(index, k):
        slot = k % 2 if isinstance(k, int) else lax.rem(k, 2)
        if index < HALVES:
            sent = region(index, False) if index < HALVES - 1 else region(HALVES - 2, True)
            source, target = grads.at[k, sent], halves.at[slot, half_rows(index)]
            step = index
        else:
            step = LEGS - 1 - index
            source = target = grads.at[k, region(step, True)]
        return pltpu.make_async_remote_copy(
            src_ref=source, dst_ref=target, send_sem=send_sem.at[slot, index], recv_sem=recv_sem.at[slot, index],
            device_id=partners[step], device_id_type=pl.DeviceIdType.MESH,
        )

    def result_copies(k):
        return [
            pltpu.make_async_copy(
                grads.at[k, pl.ds(start, count), :], outs[out].at[pl.ds(row, count), pl.ds(col, 128)], done_sem.at[k, n]
            )
            for n, (out, row, col, unit, start, count) in enumerate(
                entry for entry in unpack_blocks(width, inner, hidden) if entry[3] == k
            )
        ]

    def advance(index, k):
        slot = k % 2 if isinstance(k, int) else lax.rem(k, 2)
        if index > 0:
            stage_copy(index - 1, k).wait()
        if 0 < index <= HALVES:
            step = min(index - 1, HALVES - 2)
            own = region(step, True)
            value = grads[k, own, :] + halves[slot, half_rows(index - 1), :]
            if index == 1:
                value = value * factor_ref[0:1, :]
            grads[k, own, :] = value
            if index < HALVES:
                pl.semaphore_signal(
                    free_sem.at[k, step], inc=1, device_id=partners[step], device_id_type=pl.DeviceIdType.MESH
                )
        if index < LEGS:
            if index >= HALVES:
                pl.semaphore_wait(free_sem.at[k, LEGS - 1 - index], 1)
            stage_copy(index, k).start()
        else:
            for copy in result_copies(k):
                copy.start()

    def tick(t):
        if not linked:
            return
        for index in reversed(range(LEGS + 1)):
            u = t - RISE[index]
            if isinstance(t, int):
                if u >= 0 and u % 2 == 0 and u < 2 * units:
                    advance(index, u // 2)
            elif index < LEGS:
                ready = (u >= 0) & (u < 2 * units) & (lax.rem(u + 32, 2) == 0)
                pl.when(ready)(functools.partial(advance, index, u // 2))

    def small_copy(use, step):
        return pltpu.make_async_remote_copy(
            src_ref=small.at[use, step], dst_ref=small_in.at[use, step],
            send_sem=small_send.at[use, step], recv_sem=small_recv.at[use, step],
            device_id=plain[step], device_id_type=pl.DeviceIdType.MESH,
        )

    def small_step(use, step):
        if not linked:
            return
        if step > 0:
            small_copy(use, step - 1).wait()
            small[use, step] = small[use, step - 1] + small_in[use, step - 1]
        if step < HALVES:
            small_copy(use, step).start()

    if linked:
        total = len_ref[0]
        for i in range(1, items):
            total = total + len_ref[i]
        lane = lax.broadcasted_iota(jnp.int32, (8, width), 1)
        small[0, 0] = jnp.where(lane == group_ref[lax.axis_index("wide")], total.astype(F32), 0.0)
        small_step(0, 0)

    def set_factor():
        if not linked:
            return
        counts = small[0, HALVES]
        lane = lax.broadcasted_iota(jnp.int32, (8, width), 1)
        counts_ref[...] = counts[:, 0:128]
        roots = jnp.sqrt(counts)
        own = jnp.sum(jnp.where(lane == group_ref[lax.axis_index("wide")], roots, 0.0), axis=-1, keepdims=True)
        top = jnp.sum(counts, axis=-1, keepdims=True)
        bottom = jnp.sum(roots, axis=-1, keepdims=True) * own
        factor_ref[...] = jnp.broadcast_to(top / bottom, (8, 128))

    def scaled(values):
        if linked:
            return values * factor_ref[0:1, 0:1]
        return values * group_ref[0]

    def load(index, source, target):
        return pltpu.make_async_copy(source, target, load_sem.at[index])

    def weights(base, which, query, key, value, out):
        return [
            load(base, query, wqkv.at[which, :, pl.ds(0, inner)]),
            load(base + 1, key, wqkv.at[which, :, pl.ds(inner, inner)]),
            load(base + 2, value, wqkv.at[which, :, pl.ds(2 * inner, inner)]),
            load(base + 3, out, wout.at[which]),
        ]

    fin_load = load(0, fin_hbm, first)
    cot_load = load(1, cot_hbm, second)
    ffn_loads = [load(2, gate_hbm, gate), load(3, up_hbm, up), load(4, down_hbm, down)]
    post_load = load(5, post_hbm, xf)
    cross_weights = weights(6, 0, cq_hbm, ck_hbm, cv_hbm, co_hbm)
    self_weights = weights(10, 1, sq_hbm, sk_hbm, sv_hbm, so_hbm)
    cqkv_loads = [load(14 + j, cqkv_hbm.at[j], qkv.at[j]) for j in range(pairs)]
    cprob_loads = [load(17 + j, cprob_hbm.at[j], prob.at[j]) for j in range(pairs)]
    cmix_load = load(20, cmix_hbm, mix)
    early = [fin_load, cot_load] + ffn_loads + [post_load] + cross_weights + [cmix_load]
    for copy in early + cqkv_loads + cprob_loads + self_weights:
        copy.start()

    def item_rows(i):
        return pl.ds(pl.multiple_of(i * rows, rows), rows)

    def each_item(body, start=0, stop=items):
        def step(i, carry):
            body(i)
            return carry

        lax.fori_loop(start, stop, step, 0)

    middle = items // 2

    def emit(i, values, target):
        slot = lax.rem(i, 2)
        copy = pltpu.make_async_copy(stage.at[slot], target.at[i], out_sem.at[slot])

        @pl.when(i >= 2)
        def _():
            copy.wait()

        stage[slot] = values
        copy.start()

    def drain(target):
        for slot in range(2):
            pltpu.make_async_copy(stage.at[slot], target.at[items - 2 + slot], out_sem.at[slot]).wait()

    fin_load.wait()
    cot_load.wait()
    gain_grads[...] = jnp.zeros_like(gain_grads)

    def prepare(i):
        row = lax.broadcasted_iota(jnp.int32, (rows, width), 0)
        masked = jnp.where(row < len_ref[i], second[i], jnp.zeros((), BF16))
        second[i] = masked
        first_t[:, item_rows(i)] = first[i].T
        second_t[:, item_rows(i)] = masked.T
        din[i] = jnp.zeros((rows, width), F32)

    bounds = [items * s // (HALVES - 1) for s in range(HALVES)]
    for s in range(HALVES - 1):
        each_item(prepare, bounds[s], bounds[s + 1])
        small_step(0, s + 1)
    for copy in ffn_loads:
        copy.wait()
    post_load.wait()
    small_step(0, HALVES)
    set_factor()

    def ffn_chunk(c, carry):
        cols = pl.ds(pl.multiple_of(c * chunk, chunk), chunk)
        wg, wu, wd = gate.at[:, cols], up.at[:, cols], down.at[cols, :]

        def elementwise(i):
            source = first[i]
            g = nn(source, wg[...])
            u = nn(source, wu[...])
            dh = nt(second[i], wd[...])
            square = g * g
            t = jnp.tanh(g * (ROOT + (ROOT * CUBE) * square))
            cdf = 0.5 + 0.5 * t
            act = g * cdf
            slope = cdf + 0.5 * g * (1.0 - t * t) * (ROOT + (3.0 * ROOT * CUBE) * square)
            work[item_rows(i), 0:chunk] = (dh * u * slope).astype(BF16)
            work[item_rows(i), chunk : 2 * chunk] = (dh * act).astype(BF16)
            work[item_rows(i), 2 * chunk : 3 * chunk] = (act * u).astype(BF16)

        each_item(elementwise, 0, middle)
        tick(4 * c - 1)
        each_item(elementwise, middle, items)
        both = nn(first_t[...], work[:, 0 : 2 * chunk])
        turned = nn(second_t[...], work[:, 2 * chunk : 3 * chunk])
        for h in range(chunk // 128):
            place = (chunk // 128) * c + h
            grads[place, 0:width, :] = pair_slice(both, h)
            grads[place, width : 2 * width, :] = pair_slice(both, chunk // 128 + h)
            for m in range(width // 128):
                grads[place, 2 * width + 128 * m : 2 * width + 128 * m + 128, :] = (
                    turned[128 * m : 128 * m + 128, 128 * h : 128 * h + 128].T
                )

        tick(4 * c)

        def spread(i):
            xf[i] += nn(work[item_rows(i), 2 * chunk : 3 * chunk], wd[...])
            din[i] += nt(work[item_rows(i), 0:chunk], wg[...]) + nt(
                work[item_rows(i), chunk : 2 * chunk], wu[...]
            )

        each_item(spread, 0, middle)
        tick(4 * c + 1)
        each_item(spread, middle, items)
        tick(4 * c + 2)
        return carry

    lax.fori_loop(0, chunks, ffn_chunk, 0)
    cin_load = load(0, cin_hbm, first)
    cin_load.start()
    mem_loads = [
        load(21 + i, mem_hbm.at[i], work.at[pl.ds(i * rows, rows), pl.ds(0, width)]) for i in range(items)
    ]
    for copy in mem_loads:
        copy.start()
    each_item(lambda i: emit(i, xf[i].astype(BF16), out_hbm))
    drain(out_hbm)
    clock = 4 * chunks - 1
    tick(clock)
    post_load.start()
    cin_load.wait()
    for copy in mem_loads + cross_weights:
        copy.wait()
    cmix_load.wait()
    post_load.wait()

    def add_out_grad(place, i, branch):
        product = tn(mix[i], branch)
        for m in range(width // 128):
            grads[place, inner * m : inner * m + inner, :] += pair_slice(product, m)

    base = 2 * chunks
    grads[base] = jnp.zeros_like(grads[base])

    def cross_start(i):
        back, gain_rows = norm_back(xf[i], ffn_gain[...], din[i])
        gain_grads[2:3] += gain_rows
        total = second[i].astype(F32) + back
        din[i] = total
        branch = total.astype(BF16)
        dmix[i] = nt(branch, wout[0]).astype(BF16)
        add_out_grad(base, i, branch)
        first_t[:, item_rows(i)] = first[i].T
        second_t[:, item_rows(i)] = work[item_rows(i), 0:width].T

    each_item(cross_start)
    clock += 1
    tick(clock)
    mid_load = load(5, mid_hbm, xf)
    mid_load.start()
    text_load = load(0, text_hbm, first)
    text_load.start()

    def pair_back(j, i):
        lanes = pl.ds(pl.multiple_of(j * 128, 128), 128)
        q, k, v = qkv[j, i, :, 0:128], qkv[j, i, :, 128:256], qkv[j, i, :, 256:384]
        chance = prob[j, i]
        grad = dmix[i, :, lanes]
        product = grad.astype(F32) * mix[i, :, lanes].astype(F32)
        sums = jnp.sum(stack_heads(product, low), axis=-1, keepdims=True)
        grad2 = stack_heads(grad, low)
        score_grad = (chance.astype(F32) * (nt(grad2, v) - sums)).astype(BF16)
        dq = pick_heads(nn(score_grad, k), low) * 0.125
        work[item_rows(i), lanes] = dq.astype(BF16)
        work[item_rows(i), pl.ds(pl.multiple_of(inner + j * 128, 128), 128)] = tn(
            score_grad, stack_heads(q, low)
        ).astype(BF16)
        work[item_rows(i), pl.ds(pl.multiple_of(2 * inner + j * 128, 128), 128)] = tn(chance, grad2).astype(BF16)

    def pair_grads(place, j, inputs):
        for part in range(3):
            lanes = pl.ds(pl.multiple_of(part * inner + j * 128, 128), 128)
            grads[place, width * part : width * part + width, :] = nn(inputs[part][...], work[:, lanes])

    sqkv_loads = [load(14 + j, sqkv_hbm.at[j], qkv.at[j]) for j in range(pairs)]
    sprob_loads = [load(17 + j, sprob_hbm.at[j], prob.at[j]) for j in range(pairs)]
    for j in range(pairs):
        cqkv_loads[j].wait()
        cprob_loads[j].wait()
        each_item(functools.partial(pair_back, j), 0, middle)
        tick(clock + 1)
        each_item(functools.partial(pair_back, j), middle, items)
        pair_grads(base + 1 + j, j, (first_t, second_t, second_t))
        clock += 2
        tick(clock)
        sqkv_loads[j].start()
        sprob_loads[j].start()
    smix_load = load(20, smix_hbm, mix)
    smix_load.start()
    mid_load.wait()
    text_load.wait()
    smix_load.wait()
    for copy in self_weights:
        copy.wait()
    grads[base + 4] = jnp.zeros_like(grads[base])

    def self_start(i):
        dcross = nt(work[item_rows(i), 0:inner], wqkv[0, :, 0:inner])
        dmem = nt(work[item_rows(i), inner : 3 * inner], wqkv[0, :, inner : 3 * inner])
        emit(i, scaled(dmem).astype(BF16), mem_grad_hbm)
        back, gain_rows = norm_back(xf[i], cross_gain[...], dcross)
        gain_grads[1:2] += gain_rows
        total = din[i] + back
        din[i] = total
        branch = total.astype(BF16)
        dmix[i] = nt(branch, wout[1]).astype(BF16)
        add_out_grad(base + 4, i, branch)
        text = first[i].astype(F32)
        self_in = (text * norm_scale(text) * self_gain[...]).astype(BF16)
        first_t[:, item_rows(i)] = self_in.T

    each_item(self_start, 0, middle)
    tick(clock + 1)
    each_item(self_start, middle, items)
    clock += 2
    tick(clock)
    drain(mem_grad_hbm)
    for j in range(pairs):
        sqkv_loads[j].wait()
        sprob_loads[j].wait()
        each_item(functools.partial(pair_back, j), 0, middle)
        tick(clock + 1)
        each_item(functools.partial(pair_back, j), middle, items)
        pair_grads(base + 5 + j, j, (first_t, first_t, first_t))
        clock += 2
        tick(clock)

    def finish(i):
        dself = nt(work[item_rows(i), :], wqkv[1])
        back, gain_rows = norm_back(first[i].astype(F32), self_gain[...], dself)
        gain_grads[0:1] += gain_rows
        emit(i, scaled(din[i] + back).astype(BF16), text_grad_hbm)

    each_item(finish, 0, middle)
    tick(clock + 1)
    each_item(finish, middle, items)
    clock += 2
    tick(clock)
    drain(text_grad_hbm)
    if linked:
        small[1, 0] = scaled(gain_grads[...])
        small_step(1, 0)
        for step in range(1, max(last_tick - clock, HALVES) + 1):
            if clock + step <= last_tick:
                tick(clock + step)
            if step <= HALVES:
                small_step(1, step)
        gain_grads[...] = small[1, HALVES]
        for k in range(units):
            for copy in result_copies(k):
                copy.wait()


def backward(linked, lengths, group, gains, arrays, shapes):
    items, rows, width, inner, hidden = shapes
    pairs = HEADS // 2
    units = 2 * (hidden // 256) + 2 * (1 + pairs)
    hbm = pl.BlockSpec(memory_space=pl.ANY)
    vmem = pl.BlockSpec(memory_space=pltpu.VMEM)
    smem = pl.BlockSpec(memory_space=pltpu.SMEM)
    row_shape = jax.ShapeDtypeStruct((items, rows, width), BF16)
    gain_shape = jax.ShapeDtypeStruct((8, width), F32)
    grads_shape = (units, 3 * width, 128)
    if linked:
        natural = ([(width, inner)] * 3 + [(inner, width)]) * 2 + [(width, hidden)] * 2 + [(hidden, width)]
        out_shape = [jax.ShapeDtypeStruct(shape, F32) for shape in natural] + [
            gain_shape, jax.ShapeDtypeStruct((8, 128), F32),
        ]
        out_specs = [hbm] * len(natural) + [vmem, vmem]
        scratch = [
            pltpu.VMEM(grads_shape, F32),
            pltpu.VMEM((2, 3 * width, 128), F32),
            pltpu.VMEM((2, HALVES + 1, 8, width), F32),
            pltpu.VMEM((2, HALVES, 8, width), F32),
            pltpu.VMEM((8, 128), F32),
            pltpu.SemaphoreType.DMA((2, LEGS)),
            pltpu.SemaphoreType.DMA((2, LEGS)),
            pltpu.SemaphoreType.DMA((2, HALVES)),
            pltpu.SemaphoreType.DMA((2, HALVES)),
            pltpu.SemaphoreType.DMA((units, 6)),
            pltpu.SemaphoreType.REGULAR((units, HALVES - 1)),
        ]
        params = dict(collective_id=0, has_side_effects=True)
    else:
        out_shape, out_specs = [jax.ShapeDtypeStruct(grads_shape, F32), gain_shape], [vmem, vmem]
        scratch, params = [], {}
    return pl.pallas_call(
        functools.partial(backward_kernel, linked, items, rows, width, inner, hidden),
        in_specs=[smem, smem, vmem, vmem, vmem] + [hbm] * len(arrays),
        out_specs=[hbm, hbm, hbm] + out_specs,
        out_shape=[row_shape, row_shape, row_shape] + out_shape,
        scratch_shapes=scratch + [
            pltpu.VMEM((items, rows, width), F32),
            pltpu.VMEM((items, rows, width), F32),
            pltpu.VMEM((items, rows, width), BF16),
            pltpu.VMEM((items, rows, width), BF16),
            pltpu.VMEM((width, items * rows), BF16),
            pltpu.VMEM((width, items * rows), BF16),
            pltpu.VMEM((width, hidden), BF16),
            pltpu.VMEM((width, hidden), BF16),
            pltpu.VMEM((hidden, width), BF16),
            pltpu.VMEM((items * rows, 3 * inner), BF16),
            pltpu.VMEM((2, width, 3 * inner), BF16),
            pltpu.VMEM((2, inner, width), BF16),
            pltpu.VMEM((pairs, items, rows, 384), BF16),
            pltpu.VMEM((pairs, items, 2 * rows, rows), BF16),
            pltpu.VMEM((items, rows, inner), BF16),
            pltpu.VMEM((items, rows, inner), BF16),
            pltpu.VMEM((2, rows, width), BF16),
            pltpu.SemaphoreType.DMA((21 + items,)),
            pltpu.SemaphoreType.DMA((2,)),
        ],
        compiler_params=pltpu.CompilerParams(vmem_limit_bytes=63 * MIB, **params),
        name="backward",
    )(lengths, group, *gains, *arrays)


def unpack_blocks(width, inner, hidden):
    pairs = HEADS // 2
    blocks = []
    for b in range(hidden // 128):
        blocks.append((8, 0, 128 * b, b, 0, width))
        blocks.append((9, 0, 128 * b, b, width, width))
        for m in range(width // 128):
            blocks.append((10, 128 * b, 128 * m, b, 2 * width + 128 * m, 128))
    base = hidden // 128
    for first_out, start in ((4, base), (0, base + 1 + pairs)):
        for m in range(width // 128):
            blocks.append((first_out + 3, 0, 128 * m, start, inner * m, inner))
        for j in range(pairs):
            for part in range(3):
                blocks.append((first_out + part, 0, 128 * j, start + 1 + j, width * part, width))
    return blocks


def unpack(grads, width, inner, hidden):
    shapes = ([(width, inner)] * 3 + [(inner, width)]) * 2 + [(width, hidden)] * 2 + [(hidden, width)]
    outs = [jnp.zeros(shape, F32) for shape in shapes]
    for out, row, col, unit, start, rows in unpack_blocks(width, inner, hidden):
        outs[out] = outs[out].at[row : row + rows, col : col + 128].set(grads[unit, start : start + rows])
    return outs


def body(
    linked, text_tokens, memory, cotangent, lengths, memory_mask, group_table, self_gain, cross_gain, ffn_gain,
    self_query, self_key, self_value, self_out, cross_query, cross_key, cross_value, cross_out,
    ffn_gate, ffn_up, ffn_down,
):
    items, rows, width = text_tokens.shape
    inner, hidden = self_query.shape[1], ffn_gate.shape[1]
    gains = [gain.reshape(1, width) for gain in (self_gain, cross_gain, ffn_gain)]
    self_weights = [self_query, self_key, self_value, self_out]
    cross_weights = [cross_query, cross_key, cross_value, cross_out]
    sqkv, sprob, smix, mid, cin, cqkv, cprob, cmix, post, fin = forward(
        lengths, text_tokens, memory, memory_mask, gains, self_weights + cross_weights
    )
    arrays = (
        [fin, cotangent, ffn_gate, ffn_up, ffn_down, post, cqkv, cprob, cmix]
        + cross_weights
        + [cin, memory, mid, sqkv, sprob, smix]
        + self_weights
        + [text_tokens]
    )
    shapes = (items, rows, width, inner, hidden)
    if linked:
        layer_output, text_grad, memory_grad, *outs, gain_grads, counts = backward(
            True, lengths, group_table, gains, arrays, shapes
        )
        counts = counts[0, :GROUPS]
    else:
        places = jnp.arange(group_table.shape[0], dtype=jnp.int32)
        own_group = jnp.sum(jnp.where(places == lax.axis_index("wide"), group_table, 0))
        one_hot = (jnp.arange(GROUPS, dtype=jnp.int32) == own_group).astype(F32)
        counts = lax.psum(one_hot * jnp.sum(lengths).astype(F32), AXES)
        root_counts = jnp.sqrt(counts)
        factor = jnp.sum(one_hot * (jnp.sum(counts) / (jnp.sum(root_counts) * root_counts)))
        layer_output, text_grad, memory_grad, grads, gain_grads = backward(
            False, lengths, factor.reshape(1), gains, arrays, shapes
        )
        outs = unpack(lax.psum(factor * grads, AXES), width, inner, hidden)
        gain_grads = lax.psum(factor * gain_grads, AXES)
    return (
        layer_output, text_grad, memory_grad, gain_grads[0], gain_grads[1], gain_grads[2], *outs, counts,
    )


def solution(mesh):
    split, split2, split3, copied = P(AXES), P(AXES, None), P(AXES, None, None), P()
    linked = mesh.shape["wide"] == 8 and mesh.shape["narrow"] == 4
    return jax.shard_map(
        functools.partial(body, linked),
        mesh=mesh,
        in_specs=(split3, split3, split3, split, split2) + (copied,) * 15,
        out_specs=(split3, split3, split3) + (copied,) * 15,
        check_vma=False,
    )
```

```python
import functools

import jax
import jax.numpy as jnp
from jax import lax
from jax.experimental import pallas as pl
from jax.experimental.pallas import tpu as pltpu
from jax.sharding import PartitionSpec as P

HEADS = 6
GROUPS = 2
EPSILON = 1e-06
NEGATIVE = -1e30
F32 = jnp.float32
BF16 = jnp.bfloat16
AXES = ("wide", "narrow")
LIMIT = 44
UNROLL = 4
ROOT = 0.7978845608028654
CUBE = 0.044715
MIB = 1 << 20


def contract(left, right, left_dim, right_dim):
    return lax.dot_general(
        left, right, (((left_dim,), (right_dim,)), ((), ())), preferred_element_type=F32
    )


def nn(left, right):
    return contract(left, right, 1, 0)


def nt(left, right):
    return contract(left, right, 1, 1)


def tn(left, right):
    return contract(left, right, 0, 0)


def norm_scale(values):
    return lax.rsqrt(jnp.mean(values * values, axis=-1, keepdims=True) + EPSILON)


def norm_back(values, gain, grad):
    scale = norm_scale(values)
    unit = values * scale
    gain_rows = grad * unit
    dot = jnp.mean(gain_rows * gain, axis=-1, keepdims=True)
    return scale * (grad * gain - unit * dot), jnp.sum(gain_rows, axis=0, keepdims=True)


def low_lanes(rows):
    return lax.broadcasted_iota(jnp.int32, (rows, 128), 1) < 64


def stack_heads(pair, low):
    zero = jnp.zeros_like(pair)
    return jnp.concatenate([jnp.where(low, pair, zero), jnp.where(low, zero, pair)], axis=0)


def spread_heads(turned):
    zero = jnp.zeros_like(turned[:64])
    return jnp.concatenate(
        [jnp.concatenate([turned[:64], zero], axis=0), jnp.concatenate([zero, turned[64:]], axis=0)], axis=1
    )


def join_heads(turned):
    count = turned.shape[1] // 2
    return jnp.concatenate([turned[:64, :count], turned[64:, count:]], axis=0)


def pair_slice(values, index):
    return values[:, 128 * index : 128 * index + 128]


RISE = (0, 1, 3, 5, 7, 9, 11, 13, 15, 16)
HALVES = 5
LEGS = 2 * HALVES - 1


def exchange_plan():
    wide, narrow = lax.axis_index("wide"), lax.axis_index("narrow")
    z, y = wide // 2, wide % 2
    x, core = narrow // 2, narrow % 2
    near, far = z % 2, z // 2
    flip_x = (wide, (1 - x) * 2 + core)
    flip_y = (z * 2 + 1 - y, narrow)
    flip_core = (wide, x * 2 + 1 - core)
    flip_near = ((far * 2 + 1 - near) * 2 + y, narrow)
    flip_far = (((1 - far) * 2 + near) * 2 + y, narrow)

    def choose(first, second):
        return first + core * (second - first)

    first_flip = tuple(choose(a, b) for a, b in zip(flip_x, flip_y))
    third_flip = tuple(choose(b, a) for a, b in zip(flip_x, flip_y))
    bits = (core, choose(x, y), near, choose(y, x), far)
    partners = (flip_core, first_flip, flip_near, third_flip, flip_far)
    plain = (flip_core, flip_x, flip_near, flip_y, flip_far)
    return bits, partners, plain


def attend(query, key, value, mask, keep):
    low = low_lanes(query.shape[0])
    query = (query * 0.125).astype(BF16)
    key = key.astype(BF16)
    value = value.astype(BF16)
    mixed = []
    for j in range(HEADS // 2):
        q, k, v = pair_slice(query, j), pair_slice(key, j), pair_slice(value, j)
        scores = mask(nt(k, stack_heads(q, low)))
        top = jnp.max(scores, axis=0, keepdims=True)
        expo = jnp.exp(scores - top)
        total = jnp.sum(expo, axis=0, keepdims=True)
        prob = (expo * (1.0 / total)).astype(BF16)
        mixed.append(join_heads(nn(v.T, prob)))
        keep(j, q, k, v, prob)
    return jnp.concatenate(mixed, axis=0).astype(BF16)


def layer_kernel(
    linked, items, rows, width, inner, hidden,
    len_ref, group_ref, mask_ref, self_gain, cross_gain, ffn_gain,
    text_hbm, mem_hbm, cot_hbm, sq_hbm, sk_hbm, sv_hbm, so_hbm, cq_hbm, ck_hbm, cv_hbm, co_hbm,
    gate_hbm, up_hbm, down_hbm,
    grads, first, second, output, gain_out, counts_ref,
    sqkv_hbm, sprob_hbm, smix_hbm, mid_hbm, post_hbm,
    *rest,
):
    (xf, din, first_t, second_t, gate, up, down, work, wqkv, wout, qkv, prob, mix, dmix, gain_grads,
     load_sem, save_sem) = rest[:17]
    if linked:
        halves, small, small_in, factor_ref, send_sem, recv_sem, small_send, small_recv, free_sem = rest[17:]
    pairs = HEADS // 2
    chunk = 256
    chunks = hidden // chunk
    low = low_lanes(rows)
    units = 2 * chunks + 2 * (1 + pairs)
    last_tick = 2 * (units - 1) + RISE[-1]
    if linked:
        bits, partners, plain = exchange_plan()
        barrier = pltpu.get_barrier_semaphore()
        for device in (plain[0], plain[1], plain[2], plain[3], plain[4]):
            pl.semaphore_signal(barrier, inc=1, device_id=device, device_id_type=pl.DeviceIdType.MESH)
        pl.semaphore_wait(barrier, len(plain))

    half = 3 * width // 2

    def region(step, own):
        start = 0
        for s in range(step + 1):
            bit = bits[s] if own or s < step else 1 - bits[s]
            start = start + bit * (half >> s)
        return pl.ds(pl.multiple_of(start, 16), half >> step)

    def half_rows(step):
        size = half >> min(step, HALVES - 2)
        return pl.ds(2 * half - (2 * half >> step), size)

    def stage_copy(index, k):
        slot = k % 2 if isinstance(k, int) else lax.rem(k, 2)
        if index < HALVES:
            sent = region(index, False) if index < HALVES - 1 else region(HALVES - 2, True)
            source, target = grads.at[k, sent], halves.at[slot, half_rows(index)]
            step = index
        else:
            step = LEGS - 1 - index
            source = target = grads.at[k, region(step, True)]
        return pltpu.make_async_remote_copy(
            src_ref=source, dst_ref=target, send_sem=send_sem.at[slot, index], recv_sem=recv_sem.at[slot, index],
            device_id=partners[step], device_id_type=pl.DeviceIdType.MESH,
        )

    def advance(index, k):
        slot = k % 2 if isinstance(k, int) else lax.rem(k, 2)
        if index > 0:
            stage_copy(index - 1, k).wait()
        if 0 < index <= HALVES:
            step = min(index - 1, HALVES - 2)
            own = region(step, True)
            value = grads[k, own, :] + halves[slot, half_rows(index - 1), :]
            if index == 1:
                value = value * factor_ref[0:1, :]
            grads[k, own, :] = value
            if index < HALVES:
                pl.semaphore_signal(
                    free_sem.at[k, step], inc=1, device_id=partners[step], device_id_type=pl.DeviceIdType.MESH
                )
        if index < LEGS:
            if index >= HALVES:
                pl.semaphore_wait(free_sem.at[k, LEGS - 1 - index], 1)
            stage_copy(index, k).start()

    def tick(t):
        if not linked:
            return
        for index in reversed(range(LEGS + 1)):
            u = t - RISE[index]
            if isinstance(t, int):
                if u >= 0 and u % 2 == 0 and u < 2 * units:
                    advance(index, u // 2)
            else:
                ready = (u >= 0) & (u < 2 * units) & (lax.rem(u + 32, 2) == 0)
                pl.when(ready)(functools.partial(advance, index, u // 2))

    def small_copy(use, step):
        return pltpu.make_async_remote_copy(
            src_ref=small.at[use, step], dst_ref=small_in.at[use, step],
            send_sem=small_send.at[use, step], recv_sem=small_recv.at[use, step],
            device_id=plain[step], device_id_type=pl.DeviceIdType.MESH,
        )

    def small_step(use, step):
        if not linked:
            return
        if step > 0:
            small_copy(use, step - 1).wait()
            small[use, step] = small[use, step - 1] + small_in[use, step - 1]
        if step < HALVES:
            small_copy(use, step).start()

    if linked:
        total = len_ref[0]
        for i in range(1, items):
            total = total + len_ref[i]
        lane = lax.broadcasted_iota(jnp.int32, (8, width), 1)
        small[0, 0] = jnp.where(lane == group_ref[lax.axis_index("wide")], total.astype(F32), 0.0)
        small_step(0, 0)

    def set_factor():
        if not linked:
            return
        counts = small[0, HALVES]
        lane = lax.broadcasted_iota(jnp.int32, (8, width), 1)
        counts_ref[...] = counts[:, 0:128]
        roots = jnp.sqrt(counts)
        own = jnp.sum(jnp.where(lane == group_ref[lax.axis_index("wide")], roots, 0.0), axis=-1, keepdims=True)
        top = jnp.sum(counts, axis=-1, keepdims=True)
        bottom = jnp.sum(roots, axis=-1, keepdims=True) * own
        factor_ref[...] = jnp.broadcast_to(top / bottom, (8, 128))

    def scaled(values):
        if linked:
            return values * factor_ref[0:1, 0:1]
        return values * group_ref[0]

    def item_rows(i):
        return pl.ds(pl.multiple_of(i * rows, rows), rows)

    def each_item(body, *marks):
        several(items, body, *marks)

    def several(count, body, *marks):
        def step(i, carry):
            body(i)
            for place, time in marks:
                pl.when(i == place)(functools.partial(tick, time))
            return carry

        lax.fori_loop(0, count, step, 0)

    def load(index, source, target):
        return pltpu.make_async_copy(source, target, load_sem.at[index])

    def weights(base, which, query, key, value, out):
        return [
            load(base, query, wqkv.at[which, :, pl.ds(0, inner)]),
            load(base + 1, key, wqkv.at[which, :, pl.ds(inner, inner)]),
            load(base + 2, value, wqkv.at[which, :, pl.ds(2 * inner, inner)]),
            load(base + 3, out, wout.at[which]),
        ]

    middle = items // 2 - 1
    final = items - 1
    self_weights = weights(0, 1, sq_hbm, sk_hbm, sv_hbm, so_hbm)
    cross_weights = weights(4, 0, cq_hbm, ck_hbm, cv_hbm, co_hbm)
    ffn_loads = [load(8, gate_hbm, gate), load(9, up_hbm, up), load(10, down_hbm, down)]
    text_again = load(11, text_hbm, first)
    smix_load = load(12, smix_hbm, mix)

    def pair_loads(j):
        return [load(13 + j, sqkv_hbm.at[j], qkv.at[j]), load(13 + pairs + j, sprob_hbm.at[j], prob.at[j])]

    lists = 13 + 2 * pairs

    def text_load(i):
        return load(lists + i, text_hbm.at[i], first.at[i])

    def mem_load(i):
        return load(lists + items + i, mem_hbm.at[i], second.at[i])

    def cot_load(i):
        return load(lists + 2 * items + i, cot_hbm.at[i], second.at[i])

    def mem_again(i):
        return load(lists + 3 * items + i, mem_hbm.at[i], work.at[item_rows(i), pl.ds(0, width)])

    def mid_save(i):
        return load(lists + 4 * items + i, din.at[i], mid_hbm.at[i])

    def post_save(i):
        return load(lists + 5 * items + i, xf.at[i], post_hbm.at[i])

    def post_load(i):
        return load(lists + 6 * items + i, post_hbm.at[i], xf.at[i])

    def mid_load(i):
        return load(lists + 7 * items + i, mid_hbm.at[i], xf.at[i])

    for copy in self_weights:
        copy.start()
    for i in range(items):
        text_load(i).start()
    for copy in cross_weights:
        copy.start()
    for i in range(items):
        mem_load(i).start()
    for copy in ffn_loads:
        copy.start()
    gain_grads[...] = jnp.zeros_like(gain_grads)

    def prob_stage(u, j):
        return work.at[pl.ds(rows * (pairs * u + j), rows), pl.ds(0, 2 * rows)]

    def qkv_stage(u, j):
        return work.at[pl.ds(rows * (pairs * u + j), rows), pl.ds(2 * rows, 384)]

    def mix_stage(u):
        return work.at[pl.ds(2 * rows * pairs, inner), pl.ds(rows * u, rows)]

    def saves(u, i):
        copies = [pltpu.make_async_copy(mix_stage(u), smix_hbm.at[i], save_sem.at[u, 0])]
        for j in range(pairs):
            copies.append(pltpu.make_async_copy(qkv_stage(u, j), sqkv_hbm.at[j, i], save_sem.at[u, 1 + j]))
            copies.append(pltpu.make_async_copy(prob_stage(u, j), sprob_hbm.at[j, i], save_sem.at[u, 1 + pairs + j]))
        return copies

    for copy in self_weights:
        copy.wait()
    row = lax.broadcasted_iota(jnp.int32, (rows, 2 * rows), 0)
    col = lax.broadcasted_iota(jnp.int32, (rows, 2 * rows), 1)
    causal = row <= jnp.where(col >= rows, col - rows, col)
    turned_mask = mask_ref[...].astype(F32).T
    item_lane = lax.broadcasted_iota(jnp.int32, (rows, items), 1)

    def forward_two(b, carry):
        numbers = (2 * b, 2 * b + 1)

        @pl.when(b > 0)
        def _():
            for u in range(2):
                for copy in saves(u, 2 * b - 2 + u):
                    copy.wait()

        for i in numbers:
            text_load(i).wait()
        text = first[pl.ds(2 * b, 2)].reshape(2 * rows, width).astype(F32)
        self_in = (text * norm_scale(text) * self_gain[...]).astype(BF16)
        proj = nn(self_in, wqkv[1])
        mixed = []
        for u, i in enumerate(numbers):
            allowed = causal & (row < len_ref[i])
            mine = proj[u * rows : u * rows + rows]

            def keep(j, q, k, v, chance):
                qkv_stage(u, j)[:, 0:128] = q
                qkv_stage(u, j)[:, 128:256] = k
                qkv_stage(u, j)[:, 256:384] = v
                prob_stage(u, j)[...] = chance

            mixed.append(
                attend(
                    mine[:, :inner], mine[:, inner : 2 * inner], mine[:, 2 * inner :],
                    lambda s: jnp.where(allowed, s, NEGATIVE), keep,
                )
            )
            mix_stage(u)[...] = mixed[u]
            for copy in saves(u, i):
                copy.start()

        @pl.when(b == 0)
        def _():
            for copy in cross_weights:
                copy.wait()

        mid = text + tn(jnp.concatenate(mixed, axis=1), wout[1])
        din[pl.ds(2 * b, 2)] = mid.reshape(2, rows, width)
        for i in numbers:
            mid_save(i).start()
        cross_in = (mid * norm_scale(mid) * cross_gain[...]).astype(BF16)
        output[pl.ds(2 * b, 2)] = cross_in.reshape(2, rows, width)
        query = nn(cross_in, wqkv[0, :, 0:inner])
        for i in numbers:
            mem_load(i).wait()
        proj = nn(second[pl.ds(2 * b, 2)].reshape(2 * rows, width), wqkv[0, :, inner : 3 * inner])
        mixed = []
        for u, i in enumerate(numbers):
            cot_load(i).start()
            open_keys = jnp.sum(jnp.where(item_lane == i, turned_mask, 0.0), axis=-1, keepdims=True) > 0.0
            mine = proj[u * rows : u * rows + rows]

            def keep(j, q, k, v, chance):
                qkv[j, i, :, 0:128] = q
                qkv[j, i, :, 128:256] = k
                qkv[j, i, :, 256:384] = v
                prob[j, i] = chance

            mixed.append(
                attend(
                    query[u * rows : u * rows + rows], mine[:, :inner], mine[:, inner:],
                    lambda s: jnp.where(open_keys, s, NEGATIVE), keep,
                )
            )
            mix[i] = mixed[u]
        post = mid + tn(jnp.concatenate(mixed, axis=1), wout[0])
        xf[pl.ds(2 * b, 2)] = post.reshape(2, rows, width)
        for i in numbers:
            post_save(i).start()
        ffn_in = (post * norm_scale(post) * ffn_gain[...]).astype(BF16)
        first[pl.ds(2 * b, 2)] = ffn_in.reshape(2, rows, width)
        first_t[:, pl.ds(pl.multiple_of(2 * b * rows, 2 * rows), 2 * rows)] = ffn_in.T
        for s in range(1, HALVES):
            pl.when(b == s - 1)(functools.partial(small_step, 0, s))
        return carry

    lax.fori_loop(0, items // 2, forward_two, 0)
    for u in range(2):
        for copy in saves(u, items - 2 + u):
            copy.wait()

    def prepare(i):
        cot_load(i).wait()
        row = lax.broadcasted_iota(jnp.int32, (rows, width), 0)
        masked = jnp.where(row < len_ref[i], second[i], jnp.zeros((), BF16))
        second[i] = masked
        second_t[:, item_rows(i)] = masked.T
        mid_save(i).wait()
        post_save(i).wait()

    each_item(prepare)
    for copy in ffn_loads:
        copy.wait()
    small_step(0, HALVES)
    set_factor()

    def ffn_parts(c):
        cols = pl.ds(pl.multiple_of(c * chunk, chunk), chunk)
        return gate.at[:, cols], up.at[:, cols], down.at[cols, :]

    def ffn_grads(c):
        both = nn(first_t[...], work[:, 0 : 2 * chunk])
        turned = nn(second_t[...], work[:, 2 * chunk : 3 * chunk])
        for h in range(chunk // 128):
            place = (chunk // 128) * c + h
            grads[place, 0:width, :] = pair_slice(both, h)
            grads[place, width : 2 * width, :] = pair_slice(both, chunk // 128 + h)
            for m in range(width // 128):
                grads[place, 2 * width + 128 * m : 2 * width + 128 * m + 128, :] = (
                    turned[128 * m : 128 * m + 128, 128 * h : 128 * h + 128].T
                )

    def ffn_front(c):
        wg, wu, wd = ffn_parts(c)

        def elementwise(i):
            source = first[i]
            g = nn(source, wg[...])
            u = nn(source, wu[...])
            dh = nt(second[i], wd[...])
            square = g * g
            t = jnp.tanh(g * (ROOT + (ROOT * CUBE) * square))
            cdf = 0.5 + 0.5 * t
            act = g * cdf
            slope = cdf + 0.5 * g * (1.0 - t * t) * (ROOT + (3.0 * ROOT * CUBE) * square)
            work[item_rows(i), 0:chunk] = (dh * u * slope).astype(BF16)
            work[item_rows(i), chunk : 2 * chunk] = (dh * act).astype(BF16)
            work[item_rows(i), 2 * chunk : 3 * chunk] = (act * u).astype(BF16)

        each_item(elementwise, (middle, 4 * c - 1))
        ffn_grads(c)
        tick(4 * c)

    def back_part(c, i):
        wg, wu, wd = ffn_parts(c)
        return nt(work[item_rows(i), 0:chunk], wg[...]) + nt(work[item_rows(i), chunk : 2 * chunk], wu[...])

    def out_part(c, i):
        wg, wu, wd = ffn_parts(c)
        return xf[i] + nn(work[item_rows(i), 2 * chunk : 3 * chunk], wd[...])

    def ffn_chunk(c, carry):
        ffn_front(c)

        def spread(i):
            xf[i] = out_part(c, i)
            din[i] = jnp.where(c == 0, 0.0, din[i]) + back_part(c, i)

        each_item(spread, (middle, 4 * c + 1), (final, 4 * c + 2))
        return carry

    lax.fori_loop(0, chunks - 1, ffn_chunk, 0)
    ffn_front(chunks - 1)
    text_again.start()
    clock = 4 * (chunks - 1)

    def spread_last(i):
        din[i] += back_part(chunks - 1, i)
        done = out_part(chunks - 1, i).astype(BF16)
        first_t[:, item_rows(i)] = output[i].T
        output[i] = done
        post_load(i).start()
        mem_again(i).start()

    each_item(spread_last, (middle, clock + 1), (final, clock + 2))
    clock += 2

    def add_out_grad(place, i, branch):
        product = nn(mix[i], branch)
        for m in range(width // 128):
            grads[place, inner * m : inner * m + inner, :] += pair_slice(product, m)

    base = 2 * chunks
    grads[base] = jnp.zeros((3 * width, 128), F32)

    def cross_start(i):
        post_load(i).wait()
        back, gain_rows = norm_back(xf[i], ffn_gain[...], din[i])
        mid_load(i).start()
        gain_grads[2:3] += gain_rows
        total = second[i].astype(F32) + back
        din[i] = total
        branch = total.astype(BF16)
        dmix[i] = nt(wout[0], branch).astype(BF16)
        add_out_grad(base, i, branch)
        mem_again(i).wait()
        second_t[:, item_rows(i)] = work[item_rows(i), 0:width].T

    each_item(cross_start, (middle, clock + 1), (final, clock + 2))
    clock += 2

    def pair_terms(j, i):
        lanes = pl.ds(pl.multiple_of(j * 128, 128), 128)
        q, k, v = qkv[j, i, :, 0:128], qkv[j, i, :, 128:256], qkv[j, i, :, 256:384]
        return q, k, v, prob[j, i], dmix[i, lanes, :], mix[i, lanes, :]

    def pair_math(q, k, v, chance, grad, mixed):
        product = grad.astype(F32) * mixed.astype(F32)
        sums = jnp.concatenate(
            [jnp.sum(product[:64], axis=0, keepdims=True), jnp.sum(product[64:], axis=0, keepdims=True)], axis=1
        )
        grad2 = spread_heads(grad)
        score_grad = (chance.astype(F32) * (nn(v, grad2) - sums)).astype(BF16)
        dq = join_heads(nn(k.T, score_grad)) * 0.125
        dk = nn(score_grad, stack_heads(q, low))
        dv = nt(chance, grad2)
        return dq.astype(BF16).T, dk.astype(BF16), dv.astype(BF16)

    def pair_back(j, b):
        numbers = [UNROLL * b + u for u in range(UNROLL)]
        terms = [pair_terms(j, i) for i in numbers]
        made = [pair_math(*entry) for entry in terms]
        for i, entry in zip(numbers, made):
            for part in range(3):
                lanes = pl.ds(pl.multiple_of(part * inner + j * 128, 128), 128)
                work[item_rows(i), lanes] = entry[part]

    def pair_grads(place, j, inputs):
        for part in range(3):
            lanes = pl.ds(pl.multiple_of(part * inner + j * 128, 128), 128)
            grads[place, width * part : width * part + width, :] = nn(inputs[part][...], work[:, lanes])

    def cross_pair(j, carry):
        several(items // UNROLL, functools.partial(pair_back, j), (items // UNROLL // 2 - 1, clock + 1 + 2 * j))
        pair_grads(base + 1 + j, j, (first_t, second_t, second_t))
        for copy in pair_loads(j):
            copy.start()
        tick(clock + 2 + 2 * j)
        return carry

    lax.fori_loop(0, pairs, cross_pair, 0)
    clock += 2 * pairs
    smix_load.start()
    text_again.wait()
    smix_load.wait()
    grads[base + 1 + pairs] = jnp.zeros((3 * width, 128), F32)

    def self_start(i):
        dcross = nt(work[item_rows(i), 0:inner], wqkv[0, :, 0:inner])
        dmem = nt(work[item_rows(i), inner : 3 * inner], wqkv[0, :, inner : 3 * inner])
        second[i] = scaled(dmem).astype(BF16)
        mid_load(i).wait()
        back, gain_rows = norm_back(xf[i], cross_gain[...], dcross)
        gain_grads[1:2] += gain_rows
        total = din[i] + back
        din[i] = total
        branch = total.astype(BF16)
        dmix[i] = nt(wout[1], branch).astype(BF16)
        add_out_grad(base + 1 + pairs, i, branch)
        text = first[i].astype(F32)
        self_in = (text * norm_scale(text) * self_gain[...]).astype(BF16)
        first_t[:, item_rows(i)] = self_in.T

    each_item(self_start, (middle, clock + 1), (final, clock + 2))
    clock += 2

    def self_pair(j, carry):
        for copy in pair_loads(j):
            copy.wait()
        several(items // UNROLL, functools.partial(pair_back, j), (items // UNROLL // 2 - 1, clock + 1 + 2 * j))
        pair_grads(base + 2 + pairs + j, j, (first_t, first_t, first_t))
        tick(clock + 2 + 2 * j)
        return carry

    lax.fori_loop(0, pairs, self_pair, 0)
    clock += 2 * pairs

    def finish(i):
        dself = nt(work[item_rows(i), :], wqkv[1])
        back, gain_rows = norm_back(first[i].astype(F32), self_gain[...], dself)
        gain_grads[0:1] += gain_rows
        first[i] = scaled(din[i] + back).astype(BF16)

    each_item(finish, (middle, clock + 1), (final, clock + 2))
    clock += 2
    if linked:
        small[1, 0] = scaled(gain_grads[...])
        small_step(1, 0)
        for step in range(1, max(last_tick - clock, HALVES) + 1):
            if clock + step <= last_tick:
                tick(clock + step)
            if step <= HALVES:
                small_step(1, step)
        gain_out[...] = small[1, HALVES]
    else:
        gain_out[...] = gain_grads[...]
        counts_ref[...] = jnp.zeros_like(counts_ref)


def run_layer(linked, lengths, group, mask, gains, arrays, shapes):
    items, rows, width, inner, hidden = shapes
    pairs = HEADS // 2
    units = 2 * (hidden // 256) + 2 * (1 + pairs)
    hbm = pl.BlockSpec(memory_space=pl.ANY)
    vmem = pl.BlockSpec(memory_space=pltpu.VMEM)
    smem = pl.BlockSpec(memory_space=pltpu.SMEM)
    place_in = pltpu.VMEM if linked else jax.ShapeDtypeStruct
    scratch, params = [], {}
    if linked:
        scratch = [
            pltpu.VMEM((2, 3 * width, 128), F32),
            pltpu.VMEM((2, HALVES + 1, 8, width), F32),
            pltpu.VMEM((2, HALVES, 8, width), F32),
            pltpu.VMEM((8, 128), F32),
            pltpu.SemaphoreType.DMA((2, LEGS)),
            pltpu.SemaphoreType.DMA((2, LEGS)),
            pltpu.SemaphoreType.DMA((2, HALVES)),
            pltpu.SemaphoreType.DMA((2, HALVES)),
            pltpu.SemaphoreType.REGULAR((units, HALVES - 1)),
        ]
        params = dict(collective_id=0, has_side_effects=True)
    return pl.pallas_call(
        functools.partial(layer_kernel, linked, items, rows, width, inner, hidden),
        in_specs=[smem, smem, vmem, vmem, vmem, vmem] + [hbm] * len(arrays),
        out_specs=[vmem] * 6 + [hbm] * 5,
        out_shape=[
            place_in((units, 3 * width, 128), F32),
            place_in((items, rows, width), BF16),
            place_in((items, rows, width), BF16),
            place_in((items, rows, width), BF16),
            place_in((8, width), F32),
            place_in((8, 128), F32),
            jax.ShapeDtypeStruct((pairs, items, rows, 384), BF16),
            jax.ShapeDtypeStruct((pairs, items, rows, 2 * rows), BF16),
            jax.ShapeDtypeStruct((items, inner, rows), BF16),
            jax.ShapeDtypeStruct((items, rows, width), F32),
            jax.ShapeDtypeStruct((items, rows, width), F32),
        ],
        scratch_shapes=[
            pltpu.VMEM((items, rows, width), F32),
            pltpu.VMEM((items, rows, width), F32),
            pltpu.VMEM((width, items * rows), BF16),
            pltpu.VMEM((width, items * rows), BF16),
            pltpu.VMEM((width, hidden), BF16),
            pltpu.VMEM((width, hidden), BF16),
            pltpu.VMEM((hidden, width), BF16),
            pltpu.VMEM((items * rows, 3 * inner), BF16),
            pltpu.VMEM((2, width, 3 * inner), BF16),
            pltpu.VMEM((2, inner, width), BF16),
            pltpu.VMEM((pairs, items, rows, 384), BF16),
            pltpu.VMEM((pairs, items, rows, 2 * rows), BF16),
            pltpu.VMEM((items, inner, rows), BF16),
            pltpu.VMEM((items, inner, rows), BF16),
            pltpu.VMEM((8, width), F32),
            pltpu.SemaphoreType.DMA((13 + 2 * pairs + 8 * items,)),
            pltpu.SemaphoreType.DMA((2, 1 + 2 * pairs)),
        ] + scratch,
        compiler_params=pltpu.CompilerParams(vmem_limit_bytes=(LIMIT if linked else 63) * MIB, **params),
        name="layer",
    )(lengths, group, mask, *gains, *arrays)


def unpack_blocks(width, inner, hidden):
    pairs = HEADS // 2
    blocks = []
    for b in range(hidden // 128):
        blocks.append((8, 0, 128 * b, b, 0, width))
        blocks.append((9, 0, 128 * b, b, width, width))
        for m in range(width // 128):
            blocks.append((10, 128 * b, 128 * m, b, 2 * width + 128 * m, 128))
    base = hidden // 128
    for first_out, start in ((4, base), (0, base + 1 + pairs)):
        for m in range(width // 128):
            blocks.append((first_out + 3, 0, 128 * m, start, inner * m, inner))
        for j in range(pairs):
            for part in range(3):
                blocks.append((first_out + part, 0, 128 * j, start + 1 + j, width * part, width))
    return blocks


def unpack(grads, width, inner, hidden):
    shapes = ([(width, inner)] * 3 + [(inner, width)]) * 2 + [(width, hidden)] * 2 + [(hidden, width)]
    outs = [jnp.zeros(shape, F32) for shape in shapes]
    for out, row, col, unit, start, rows in unpack_blocks(width, inner, hidden):
        outs[out] = outs[out].at[row : row + rows, col : col + 128].set(grads[unit, start : start + rows])
    return outs


def place_kernel(blocks, grads, text_grad, memory_grad, output, gains, counts, *refs):
    outs, (gain_outs, count_out, sem) = refs[:-5], (refs[-5:-2], refs[-2], refs[-1])
    copies = [
        pltpu.make_async_copy(
            grads.at[unit, pl.ds(start, rows), :], outs[3 + out].at[pl.ds(row, rows), pl.ds(col, 128)], sem.at[n]
        )
        for n, (out, row, col, unit, start, rows) in enumerate(blocks)
    ]
    for n, source in enumerate((output, text_grad, memory_grad)):
        copies.append(pltpu.make_async_copy(source, outs[n], sem.at[len(blocks) + n]))
    for copy in copies:
        copy.start()
    for n in range(3):
        gain_outs[n][...] = gains[n]
    for n in range(GROUPS):
        count_out[n] = jnp.sum(counts[0:1, n : n + 1])
    for copy in copies:
        copy.wait()


def place(arrays, width, inner, hidden):
    blocks = unpack_blocks(width, inner, hidden)
    rows = arrays[1].shape
    shapes = ([(width, inner)] * 3 + [(inner, width)]) * 2 + [(width, hidden)] * 2 + [(hidden, width)]
    hbm, vmem = pl.BlockSpec(memory_space=pl.ANY), pl.BlockSpec(memory_space=pltpu.VMEM)
    return pl.pallas_call(
        functools.partial(place_kernel, blocks),
        in_specs=[vmem] * 6,
        out_specs=[hbm] * (3 + len(shapes)) + [vmem] * 3 + [pl.BlockSpec(memory_space=pltpu.SMEM)],
        out_shape=[jax.ShapeDtypeStruct(rows, BF16)] * 3
        + [jax.ShapeDtypeStruct(shape, F32) for shape in shapes]
        + [jax.ShapeDtypeStruct((width,), F32)] * 3
        + [jax.ShapeDtypeStruct((GROUPS,), F32)],
        scratch_shapes=[pltpu.SemaphoreType.DMA((len(blocks) + 3,))],
        compiler_params=pltpu.CompilerParams(vmem_limit_bytes=1 * MIB),
        name="place",
    )(*[pltpu.with_memory_space_constraint(array, pltpu.VMEM) for array in arrays])


def body(
    linked, text_tokens, memory, cotangent, lengths, memory_mask, group_table, self_gain, cross_gain, ffn_gain,
    self_query, self_key, self_value, self_out, cross_query, cross_key, cross_value, cross_out,
    ffn_gate, ffn_up, ffn_down,
):
    items, rows, width = text_tokens.shape
    inner, hidden = self_query.shape[1], ffn_gate.shape[1]
    gains = [gain.reshape(1, width) for gain in (self_gain, cross_gain, ffn_gain)]
    arrays = [
        text_tokens, memory, cotangent, self_query, self_key, self_value, self_out, cross_query, cross_key,
        cross_value, cross_out, ffn_gate, ffn_up, ffn_down,
    ]
    shapes = (items, rows, width, inner, hidden)
    if linked:
        made = run_layer(True, lengths, group_table, memory_mask, gains, arrays, shapes)
        layer_output, text_grad, memory_grad, *outs = place(made[:6], width, inner, hidden)
        return (layer_output, text_grad, memory_grad, *outs[-4:-1], *outs[:-4], outs[-1])
    places = jnp.arange(group_table.shape[0], dtype=jnp.int32)
    own_group = jnp.sum(jnp.where(places == lax.axis_index("wide"), group_table, 0))
    one_hot = (jnp.arange(GROUPS, dtype=jnp.int32) == own_group).astype(F32)
    counts = lax.psum(one_hot * jnp.sum(lengths).astype(F32), AXES)
    root_counts = jnp.sqrt(counts)
    factor = jnp.sum(one_hot * (jnp.sum(counts) / (jnp.sum(root_counts) * root_counts)))
    grads, text_grad, memory_grad, layer_output, gain_grads, *unused = run_layer(
        False, lengths, factor.reshape(1), memory_mask, gains, arrays, shapes
    )
    outs = unpack(lax.psum(factor * grads, AXES), width, inner, hidden)
    gain_grads = lax.psum(factor * gain_grads, AXES)
    return (
        layer_output, text_grad, memory_grad, gain_grads[0], gain_grads[1], gain_grads[2], *outs, counts,
    )


def solution(mesh):
    split, split2, split3, copied = P(AXES), P(AXES, None), P(AXES, None, None), P()
    linked = mesh.shape["wide"] == 8 and mesh.shape["narrow"] == 4
    return jax.shard_map(
        functools.partial(body, linked),
        mesh=mesh,
        in_specs=(split3, split3, split3, split, split2) + (copied,) * 15,
        out_specs=(split3, split3, split3) + (copied,) * 15,
        check_vma=False,
    )
```

```python
import functools

import jax
import jax.numpy as jnp
from jax import lax
from jax.experimental import pallas as pl
from jax.experimental.pallas import tpu as pltpu
from jax.sharding import PartitionSpec as P

HEADS = 6
GROUPS = 2
EPSILON = 1e-06
NEGATIVE = -1e30
F32 = jnp.float32
BF16 = jnp.bfloat16
AXES = ("wide", "narrow")
LIMIT = 44
UNROLL = 4
ROOT = 0.7978845608028654
CUBE = 0.044715
MIB = 1 << 20


def contract(left, right, left_dim, right_dim):
    return lax.dot_general(
        left, right, (((left_dim,), (right_dim,)), ((), ())), preferred_element_type=F32
    )


def nn(left, right):
    return contract(left, right, 1, 0)


def nt(left, right):
    return contract(left, right, 1, 1)


def tn(left, right):
    return contract(left, right, 0, 0)


def norm_scale(values):
    return lax.rsqrt(jnp.mean(values * values, axis=-1, keepdims=True) + EPSILON)


def norm_back(values, gain, grad):
    scale = norm_scale(values)
    unit = values * scale
    gain_rows = grad * unit
    dot = jnp.mean(gain_rows * gain, axis=-1, keepdims=True)
    return scale * (grad * gain - unit * dot), jnp.sum(gain_rows, axis=0, keepdims=True)


def low_lanes(rows):
    return lax.broadcasted_iota(jnp.int32, (rows, 128), 1) < 64


def stack_heads(pair, low):
    zero = jnp.zeros_like(pair)
    return jnp.concatenate([jnp.where(low, pair, zero), jnp.where(low, zero, pair)], axis=0)


def spread_heads(turned):
    zero = jnp.zeros_like(turned[:64])
    return jnp.concatenate(
        [jnp.concatenate([turned[:64], zero], axis=0), jnp.concatenate([zero, turned[64:]], axis=0)], axis=1
    )


def join_heads(turned):
    count = turned.shape[1] // 2
    return jnp.concatenate([turned[:64, :count], turned[64:, count:]], axis=0)


def pair_slice(values, index):
    return values[:, 128 * index : 128 * index + 128]


RISE = (0, 1, 3, 5, 7, 9, 10, 12, 14, 15)
HALVES = 5
LEGS = 2 * HALVES - 1


def exchange_plan():
    wide, narrow = lax.axis_index("wide"), lax.axis_index("narrow")
    z, y = wide // 2, wide % 2
    x, core = narrow // 2, narrow % 2
    near, far = z % 2, z // 2
    flip_x = (wide, (1 - x) * 2 + core)
    flip_y = (z * 2 + 1 - y, narrow)
    flip_core = (wide, x * 2 + 1 - core)
    flip_near = ((far * 2 + 1 - near) * 2 + y, narrow)
    flip_far = (((1 - far) * 2 + near) * 2 + y, narrow)

    def choose(first, second):
        return first + core * (second - first)

    first_flip = tuple(choose(a, b) for a, b in zip(flip_x, flip_y))
    third_flip = tuple(choose(b, a) for a, b in zip(flip_x, flip_y))
    bits = (core, choose(x, y), near, choose(y, x), far)
    partners = (flip_core, first_flip, flip_near, third_flip, flip_far)
    plain = (flip_core, flip_x, flip_near, flip_y, flip_far)
    return bits, partners, plain


def attend(query, key, value, mask, keep):
    low = low_lanes(query.shape[0])
    query = (query * 0.125).astype(BF16)
    key = key.astype(BF16)
    value = value.astype(BF16)
    mixed = []
    for j in range(HEADS // 2):
        q, k, v = pair_slice(query, j), pair_slice(key, j), pair_slice(value, j)
        scores = mask(nt(k, stack_heads(q, low)))
        top = jnp.max(scores, axis=0, keepdims=True)
        expo = jnp.exp(scores - top)
        total = jnp.sum(expo, axis=0, keepdims=True)
        prob = (expo * (1.0 / total)).astype(BF16)
        mixed.append(join_heads(nn(v.T, prob)))
        keep(j, q, k, v, prob)
    return jnp.concatenate(mixed, axis=0).astype(BF16)


def layer_kernel(
    linked, items, rows, width, inner, hidden,
    len_ref, group_ref, mask_ref, self_gain, cross_gain, ffn_gain,
    text_hbm, mem_hbm, cot_hbm, sq_hbm, sk_hbm, sv_hbm, so_hbm, cq_hbm, ck_hbm, cv_hbm, co_hbm,
    gate_hbm, up_hbm, down_hbm,
    grads, first, second, output, gain_out, counts_ref,
    sqkv_hbm, sprob_hbm, smix_hbm, mid_hbm, post_hbm,
    *rest,
):
    (xf, din, first_t, second_t, gate, up, down, work, wqkv, wout, qkv, prob, mix, dmix, gain_grads,
     load_sem, save_sem) = rest[:17]
    if linked:
        halves, small, small_in, factor_ref, send_sem, recv_sem, small_send, small_recv, free_sem = rest[17:]
    pairs = HEADS // 2
    chunk = 256
    chunks = hidden // chunk
    low = low_lanes(rows)
    units = 2 * chunks + 2 * (1 + pairs)
    last_tick = 2 * (units - 1) + RISE[-1]
    if linked:
        bits, partners, plain = exchange_plan()
        barrier = pltpu.get_barrier_semaphore()
        for device in (plain[0], plain[1], plain[2], plain[3], plain[4]):
            pl.semaphore_signal(barrier, inc=1, device_id=device, device_id_type=pl.DeviceIdType.MESH)
        pl.semaphore_wait(barrier, len(plain))

    half = 3 * width // 2

    def region(step, own):
        start = 0
        for s in range(step + 1):
            bit = bits[s] if own or s < step else 1 - bits[s]
            start = start + bit * (half >> s)
        return pl.ds(pl.multiple_of(start, 16), half >> step)

    def half_rows(step):
        size = half >> min(step, HALVES - 2)
        return pl.ds(2 * half - (2 * half >> step), size)

    def stage_copy(index, k):
        slot = k % 2 if isinstance(k, int) else lax.rem(k, 2)
        if index < HALVES:
            sent = region(index, False) if index < HALVES - 1 else region(HALVES - 2, True)
            source, target = grads.at[k, sent], halves.at[slot, half_rows(index)]
            step = index
        else:
            step = LEGS - 1 - index
            source = target = grads.at[k, region(step, True)]
        return pltpu.make_async_remote_copy(
            src_ref=source, dst_ref=target, send_sem=send_sem.at[slot, index], recv_sem=recv_sem.at[slot, index],
            device_id=partners[step], device_id_type=pl.DeviceIdType.MESH,
        )

    def advance(index, k):
        slot = k % 2 if isinstance(k, int) else lax.rem(k, 2)
        if index > 0:
            stage_copy(index - 1, k).wait()
        if 0 < index <= HALVES:
            step = min(index - 1, HALVES - 2)
            own = region(step, True)
            value = grads[k, own, :] + halves[slot, half_rows(index - 1), :]
            if index == 1:
                value = value * factor_ref[0:1, :]
            grads[k, own, :] = value
            if index < HALVES:
                pl.semaphore_signal(
                    free_sem.at[k, step], inc=1, device_id=partners[step], device_id_type=pl.DeviceIdType.MESH
                )
        if index < LEGS:
            if index >= HALVES:
                pl.semaphore_wait(free_sem.at[k, LEGS - 1 - index], 1)
            stage_copy(index, k).start()

    def tick(t):
        if not linked:
            return
        for index in reversed(range(LEGS + 1)):
            u = t - RISE[index]
            if isinstance(t, int):
                if u >= 0 and u % 2 == 0 and u < 2 * units:
                    advance(index, u // 2)
            else:
                ready = (u >= 0) & (u < 2 * units) & (lax.rem(u + 32, 2) == 0)
                pl.when(ready)(functools.partial(advance, index, u // 2))

    def small_copy(use, step):
        return pltpu.make_async_remote_copy(
            src_ref=small.at[use, step], dst_ref=small_in.at[use, step],
            send_sem=small_send.at[use, step], recv_sem=small_recv.at[use, step],
            device_id=plain[step], device_id_type=pl.DeviceIdType.MESH,
        )

    def small_step(use, step):
        if not linked:
            return
        if step > 0:
            small_copy(use, step - 1).wait()
            small[use, step] = small[use, step - 1] + small_in[use, step - 1]
        if step < HALVES:
            small_copy(use, step).start()

    if linked:
        total = len_ref[0]
        for i in range(1, items):
            total = total + len_ref[i]
        lane = lax.broadcasted_iota(jnp.int32, (8, width), 1)
        small[0, 0] = jnp.where(lane == group_ref[lax.axis_index("wide")], total.astype(F32), 0.0)
        small_step(0, 0)

    def set_factor():
        if not linked:
            return
        counts = small[0, HALVES]
        lane = lax.broadcasted_iota(jnp.int32, (8, width), 1)
        counts_ref[...] = counts[:, 0:128]
        roots = jnp.sqrt(counts)
        own = jnp.sum(jnp.where(lane == group_ref[lax.axis_index("wide")], roots, 0.0), axis=-1, keepdims=True)
        top = jnp.sum(counts, axis=-1, keepdims=True)
        bottom = jnp.sum(roots, axis=-1, keepdims=True) * own
        factor_ref[...] = jnp.broadcast_to(top / bottom, (8, 128))

    def scaled(values):
        if linked:
            return values * factor_ref[0:1, 0:1]
        return values * group_ref[0]

    def item_rows(i):
        return pl.ds(pl.multiple_of(i * rows, rows), rows)

    def each_item(body, *marks):
        several(items, body, *marks)

    def several(count, body, *marks):
        def step(i, carry):
            body(i)
            for place, time in marks:
                pl.when(i == place)(functools.partial(tick, time))
            return carry

        lax.fori_loop(0, count, step, 0)

    def load(index, source, target):
        return pltpu.make_async_copy(source, target, load_sem.at[index])

    def weights(base, which, query, key, value, out):
        return [
            load(base, query, wqkv.at[which, :, pl.ds(0, inner)]),
            load(base + 1, key, wqkv.at[which, :, pl.ds(inner, inner)]),
            load(base + 2, value, wqkv.at[which, :, pl.ds(2 * inner, inner)]),
            load(base + 3, out, wout.at[which]),
        ]

    middle = items // 2 - 1
    final = items - 1
    self_weights = weights(0, 1, sq_hbm, sk_hbm, sv_hbm, so_hbm)
    cross_weights = weights(4, 0, cq_hbm, ck_hbm, cv_hbm, co_hbm)
    ffn_loads = [load(8, gate_hbm, gate), load(9, up_hbm, up), load(10, down_hbm, down)]
    text_again = load(11, text_hbm, first)
    smix_load = load(12, smix_hbm, mix)

    def pair_loads(j):
        return [load(13 + j, sqkv_hbm.at[j], qkv.at[j]), load(13 + pairs + j, sprob_hbm.at[j], prob.at[j])]

    lists = 13 + 2 * pairs

    def text_load(i):
        return load(lists + i, text_hbm.at[i], first.at[i])

    def mem_load(i):
        return load(lists + items + i, mem_hbm.at[i], second.at[i])

    def cot_load(i):
        return load(lists + 2 * items + i, cot_hbm.at[i], second.at[i])

    def mem_again(i):
        return load(lists + 3 * items + i, mem_hbm.at[i], work.at[item_rows(i), pl.ds(0, width)])

    def mid_save(i):
        return load(lists + 4 * items + i, din.at[i], mid_hbm.at[i])

    def post_save(i):
        return load(lists + 5 * items + i, xf.at[i], post_hbm.at[i])

    def post_load(i):
        return load(lists + 6 * items + i, post_hbm.at[i], xf.at[i])

    def mid_load(i):
        return load(lists + 7 * items + i, mid_hbm.at[i], xf.at[i])

    for copy in self_weights:
        copy.start()
    for i in range(items):
        text_load(i).start()
    for copy in cross_weights:
        copy.start()
    for i in range(items):
        mem_load(i).start()
    for copy in ffn_loads:
        copy.start()
    gain_grads[...] = jnp.zeros_like(gain_grads)

    def prob_stage(u, j):
        return work.at[pl.ds(rows * (pairs * u + j), rows), pl.ds(0, 2 * rows)]

    def qkv_stage(u, j):
        return work.at[pl.ds(rows * (pairs * u + j), rows), pl.ds(2 * rows, 384)]

    def mix_stage(u):
        return work.at[pl.ds(2 * rows * pairs, inner), pl.ds(rows * u, rows)]

    def saves(u, i):
        copies = [pltpu.make_async_copy(mix_stage(u), smix_hbm.at[i], save_sem.at[u, 0])]
        for j in range(pairs):
            copies.append(pltpu.make_async_copy(qkv_stage(u, j), sqkv_hbm.at[j, i], save_sem.at[u, 1 + j]))
            copies.append(pltpu.make_async_copy(prob_stage(u, j), sprob_hbm.at[j, i], save_sem.at[u, 1 + pairs + j]))
        return copies

    for copy in self_weights:
        copy.wait()
    row = lax.broadcasted_iota(jnp.int32, (rows, 2 * rows), 0)
    col = lax.broadcasted_iota(jnp.int32, (rows, 2 * rows), 1)
    causal = row <= jnp.where(col >= rows, col - rows, col)
    turned_mask = mask_ref[...].astype(F32).T
    item_lane = lax.broadcasted_iota(jnp.int32, (rows, items), 1)

    def forward_two(b, carry):
        numbers = (2 * b, 2 * b + 1)

        @pl.when(b > 0)
        def _():
            for u in range(2):
                for copy in saves(u, 2 * b - 2 + u):
                    copy.wait()

        for i in numbers:
            text_load(i).wait()
        text = first[pl.ds(2 * b, 2)].reshape(2 * rows, width).astype(F32)
        self_in = (text * norm_scale(text) * self_gain[...]).astype(BF16)
        proj = nn(self_in, wqkv[1])
        mixed = []
        for u, i in enumerate(numbers):
            allowed = causal & (row < len_ref[i])
            mine = proj[u * rows : u * rows + rows]

            def keep(j, q, k, v, chance):
                qkv_stage(u, j)[:, 0:128] = q
                qkv_stage(u, j)[:, 128:256] = k
                qkv_stage(u, j)[:, 256:384] = v
                prob_stage(u, j)[...] = chance

            mixed.append(
                attend(
                    mine[:, :inner], mine[:, inner : 2 * inner], mine[:, 2 * inner :],
                    lambda s: jnp.where(allowed, s, NEGATIVE), keep,
                )
            )
            mix_stage(u)[...] = mixed[u]
            for copy in saves(u, i):
                copy.start()

        @pl.when(b == 0)
        def _():
            for copy in cross_weights:
                copy.wait()

        mid = text + tn(jnp.concatenate(mixed, axis=1), wout[1])
        din[pl.ds(2 * b, 2)] = mid.reshape(2, rows, width)
        for i in numbers:
            mid_save(i).start()
        cross_in = (mid * norm_scale(mid) * cross_gain[...]).astype(BF16)
        output[pl.ds(2 * b, 2)] = cross_in.reshape(2, rows, width)
        query = nn(cross_in, wqkv[0, :, 0:inner])
        for i in numbers:
            mem_load(i).wait()
        proj = nn(second[pl.ds(2 * b, 2)].reshape(2 * rows, width), wqkv[0, :, inner : 3 * inner])
        mixed = []
        for u, i in enumerate(numbers):
            cot_load(i).start()
            open_keys = jnp.sum(jnp.where(item_lane == i, turned_mask, 0.0), axis=-1, keepdims=True) > 0.0
            mine = proj[u * rows : u * rows + rows]

            def keep(j, q, k, v, chance):
                qkv[j, i, :, 0:128] = q
                qkv[j, i, :, 128:256] = k
                qkv[j, i, :, 256:384] = v
                prob[j, i] = chance

            mixed.append(
                attend(
                    query[u * rows : u * rows + rows], mine[:, :inner], mine[:, inner:],
                    lambda s: jnp.where(open_keys, s, NEGATIVE), keep,
                )
            )
            mix[i] = mixed[u]
        post = mid + tn(jnp.concatenate(mixed, axis=1), wout[0])
        xf[pl.ds(2 * b, 2)] = post.reshape(2, rows, width)
        for i in numbers:
            post_save(i).start()
        ffn_in = (post * norm_scale(post) * ffn_gain[...]).astype(BF16)
        first[pl.ds(2 * b, 2)] = ffn_in.reshape(2, rows, width)
        first_t[:, pl.ds(pl.multiple_of(2 * b * rows, 2 * rows), 2 * rows)] = ffn_in.T
        for s in range(1, HALVES):
            pl.when(b == s - 1)(functools.partial(small_step, 0, s))
        return carry

    lax.fori_loop(0, items // 2, forward_two, 0)
    for u in range(2):
        for copy in saves(u, items - 2 + u):
            copy.wait()

    def prepare(i):
        cot_load(i).wait()
        row = lax.broadcasted_iota(jnp.int32, (rows, width), 0)
        masked = jnp.where(row < len_ref[i], second[i], jnp.zeros((), BF16))
        second[i] = masked
        second_t[:, item_rows(i)] = masked.T
        mid_save(i).wait()
        post_save(i).wait()

    each_item(prepare)
    for copy in ffn_loads:
        copy.wait()
    small_step(0, HALVES)
    set_factor()

    def ffn_parts(c):
        cols = pl.ds(c * chunk, chunk)
        return gate.at[:, cols], up.at[:, cols], down.at[cols, :]

    def ffn_grads(c):
        both = nn(first_t[...], work[:, 0 : 2 * chunk])
        turned = nn(second_t[...], work[:, 2 * chunk : 3 * chunk])
        for h in range(chunk // 128):
            place = (chunk // 128) * c + h
            grads[place, 0:width, :] = pair_slice(both, h)
            grads[place, width : 2 * width, :] = pair_slice(both, chunk // 128 + h)
            for m in range(width // 128):
                grads[place, 2 * width + 128 * m : 2 * width + 128 * m + 128, :] = (
                    turned[128 * m : 128 * m + 128, 128 * h : 128 * h + 128].T
                )

    def ffn_front(c):
        wg, wu, wd = ffn_parts(c)

        def elementwise(i):
            source = first[i]
            g = nn(source, wg[...])
            u = nn(source, wu[...])
            dh = nt(second[i], wd[...])
            square = g * g
            t = jnp.tanh(g * (ROOT + (ROOT * CUBE) * square))
            cdf = 0.5 + 0.5 * t
            act = g * cdf
            slope = cdf + 0.5 * g * (1.0 - t * t) * (ROOT + (3.0 * ROOT * CUBE) * square)
            work[item_rows(i), 0:chunk] = (dh * u * slope).astype(BF16)
            work[item_rows(i), chunk : 2 * chunk] = (dh * act).astype(BF16)
            work[item_rows(i), 2 * chunk : 3 * chunk] = (act * u).astype(BF16)

        each_item(elementwise, (middle, 4 * c - 1))
        ffn_grads(c)
        tick(4 * c)

    def back_part(c, i):
        wg, wu, wd = ffn_parts(c)
        return nt(work[item_rows(i), 0:chunk], wg[...]) + nt(work[item_rows(i), chunk : 2 * chunk], wu[...])

    def out_part(c, i):
        wg, wu, wd = ffn_parts(c)
        return xf[i] + nn(work[item_rows(i), 2 * chunk : 3 * chunk], wd[...])

    def ffn_chunk(c, carry):
        ffn_front(c)

        def spread(i):
            xf[i] = out_part(c, i)
            din[i] = back_part(c, i) if c == 0 else din[i] + back_part(c, i)

        each_item(spread, (middle, 4 * c + 1), (final, 4 * c + 2))
        return carry

    for c in range(chunks - 1):
        ffn_chunk(c, 0)
    ffn_front(chunks - 1)
    text_again.start()
    clock = 4 * (chunks - 1)

    def spread_last(i):
        din[i] += back_part(chunks - 1, i)
        done = out_part(chunks - 1, i).astype(BF16)
        first_t[:, item_rows(i)] = output[i].T
        output[i] = done
        post_load(i).start()
        mem_again(i).start()

    each_item(spread_last, (middle, clock + 1), (final, clock + 2))
    clock += 2

    def two(b):
        return pl.ds(2 * b, 2)

    def two_rows(b):
        return pl.ds(pl.multiple_of(2 * b * rows, 2 * rows), 2 * rows)

    def flat(values):
        return values.reshape(2 * rows, width)

    def send_back(place, b, total, which):
        din[two(b)] = total.reshape(2, rows, width)
        branch = total.astype(BF16)
        turned = nt(wout[which], branch).astype(BF16)
        dmix[2 * b] = turned[:, :rows]
        dmix[2 * b + 1] = turned[:, rows:]
        product = nn(mix[2 * b], branch[:rows]) + nn(mix[2 * b + 1], branch[rows:])
        for m in range(width // 128):
            grads[place, inner * m : inner * m + inner, :] += pair_slice(product, m)

    base = 2 * chunks
    grads[base] = jnp.zeros((3 * width, 128), F32)

    def cross_start(b):
        for u in range(2):
            post_load(2 * b + u).wait()
        back, gain_rows = norm_back(flat(xf[two(b)]), ffn_gain[...], flat(din[two(b)]))
        for u in range(2):
            mid_load(2 * b + u).start()
        gain_grads[2:3] += gain_rows
        send_back(base, b, flat(second[two(b)]).astype(F32) + back, 0)
        for u in range(2):
            mem_again(2 * b + u).wait()
        second_t[:, two_rows(b)] = work[two_rows(b), 0:width].T

    several(items // 2, cross_start, (items // 4 - 1, clock + 1), (items // 2 - 1, clock + 2))
    clock += 2

    def pair_terms(j, i):
        lanes = pl.ds(j * 128, 128)
        q, k, v = qkv[j, i, :, 0:128], qkv[j, i, :, 128:256], qkv[j, i, :, 256:384]
        return q, k, v, prob[j, i], dmix[i, lanes, :], mix[i, lanes, :]

    def pair_math(q, k, v, chance, grad, mixed):
        product = grad.astype(F32) * mixed.astype(F32)
        sums = jnp.concatenate(
            [jnp.sum(product[:64], axis=0, keepdims=True), jnp.sum(product[64:], axis=0, keepdims=True)], axis=1
        )
        grad2 = spread_heads(grad)
        score_grad = (chance.astype(F32) * (nn(v, grad2) - sums)).astype(BF16)
        dq = join_heads(nn(k.T, score_grad)) * 0.125
        dk = nn(score_grad, stack_heads(q, low))
        dv = nt(chance, grad2)
        return dq.astype(BF16).T, dk.astype(BF16), dv.astype(BF16)

    def pair_back(j, b):
        numbers = [UNROLL * b + u for u in range(UNROLL)]
        terms = [pair_terms(j, i) for i in numbers]
        made = [pair_math(*entry) for entry in terms]
        for i, entry in zip(numbers, made):
            for part in range(3):
                lanes = pl.ds(part * inner + j * 128, 128)
                work[item_rows(i), lanes] = entry[part]

    def pair_grads(place, j, inputs):
        for part in range(3):
            lanes = pl.ds(part * inner + j * 128, 128)
            grads[place, width * part : width * part + width, :] = nn(inputs[part][...], work[:, lanes])

    def cross_pair(j, carry):
        several(items // UNROLL, functools.partial(pair_back, j), (items // UNROLL // 2 - 1, clock + 1 + 2 * j))
        pair_grads(base + 1 + j, j, (first_t, second_t, second_t))
        for copy in pair_loads(j):
            copy.start()
        tick(clock + 2 + 2 * j)
        return carry

    for j in range(pairs):
        cross_pair(j, 0)
    clock += 2 * pairs
    smix_load.start()
    text_again.wait()
    smix_load.wait()
    grads[base + 1 + pairs] = jnp.zeros((3 * width, 128), F32)

    def self_start(b):
        dcross = nt(work[two_rows(b), 0:inner], wqkv[0, :, 0:inner])
        dmem = nt(work[two_rows(b), inner : 3 * inner], wqkv[0, :, inner : 3 * inner])
        second[two(b)] = scaled(dmem).astype(BF16).reshape(2, rows, width)
        for u in range(2):
            mid_load(2 * b + u).wait()
        back, gain_rows = norm_back(flat(xf[two(b)]), cross_gain[...], dcross)
        gain_grads[1:2] += gain_rows
        send_back(base + 1 + pairs, b, flat(din[two(b)]) + back, 1)
        text = flat(first[two(b)]).astype(F32)
        self_in = (text * norm_scale(text) * self_gain[...]).astype(BF16)
        first_t[:, two_rows(b)] = self_in.T

    several(items // 2, self_start, (items // 4 - 1, clock + 1), (items // 2 - 1, clock + 2))
    clock += 2

    def self_pair(j, carry):
        for copy in pair_loads(j):
            copy.wait()
        several(items // UNROLL, functools.partial(pair_back, j), (items // UNROLL // 2 - 1, clock + 1 + 2 * j))
        pair_grads(base + 2 + pairs + j, j, (first_t, first_t, first_t))
        tick(clock + 2 + 2 * j)
        return carry

    for j in range(pairs):
        self_pair(j, 0)
    clock += 2 * pairs

    def finish(b):
        dself = nt(work[two_rows(b), :], wqkv[1])
        back, gain_rows = norm_back(flat(first[two(b)]).astype(F32), self_gain[...], dself)
        gain_grads[0:1] += gain_rows
        made = scaled(flat(din[two(b)]) + back).astype(BF16)
        first[two(b)] = made.reshape(2, rows, width)

    several(items // 2, finish, (items // 4 - 1, clock + 1), (items // 2 - 1, clock + 2))
    clock += 2
    if linked:
        small[1, 0] = scaled(gain_grads[...])
        small_step(1, 0)
        for step in range(1, max(last_tick - clock, HALVES) + 1):
            if clock + step <= last_tick:
                tick(clock + step)
            if step <= HALVES:
                small_step(1, step)
        gain_out[...] = small[1, HALVES]
    else:
        gain_out[...] = gain_grads[...]
        counts_ref[...] = jnp.zeros_like(counts_ref)


def run_layer(linked, lengths, group, mask, gains, arrays, shapes):
    items, rows, width, inner, hidden = shapes
    pairs = HEADS // 2
    units = 2 * (hidden // 256) + 2 * (1 + pairs)
    hbm = pl.BlockSpec(memory_space=pl.ANY)
    vmem = pl.BlockSpec(memory_space=pltpu.VMEM)
    smem = pl.BlockSpec(memory_space=pltpu.SMEM)
    place_in = pltpu.VMEM if linked else jax.ShapeDtypeStruct
    scratch, params = [], {}
    if linked:
        scratch = [
            pltpu.VMEM((2, 3 * width, 128), F32),
            pltpu.VMEM((2, HALVES + 1, 8, width), F32),
            pltpu.VMEM((2, HALVES, 8, width), F32),
            pltpu.VMEM((8, 128), F32),
            pltpu.SemaphoreType.DMA((2, LEGS)),
            pltpu.SemaphoreType.DMA((2, LEGS)),
            pltpu.SemaphoreType.DMA((2, HALVES)),
            pltpu.SemaphoreType.DMA((2, HALVES)),
            pltpu.SemaphoreType.REGULAR((units, HALVES - 1)),
        ]
        params = dict(collective_id=0, has_side_effects=True)
    return pl.pallas_call(
        functools.partial(layer_kernel, linked, items, rows, width, inner, hidden),
        in_specs=[smem, smem, vmem, vmem, vmem, vmem] + [hbm] * len(arrays),
        out_specs=[vmem] * 6 + [hbm] * 5,
        out_shape=[
            place_in((units, 3 * width, 128), F32),
            place_in((items, rows, width), BF16),
            place_in((items, rows, width), BF16),
            place_in((items, rows, width), BF16),
            place_in((8, width), F32),
            place_in((8, 128), F32),
            jax.ShapeDtypeStruct((pairs, items, rows, 384), BF16),
            jax.ShapeDtypeStruct((pairs, items, rows, 2 * rows), BF16),
            jax.ShapeDtypeStruct((items, inner, rows), BF16),
            jax.ShapeDtypeStruct((items, rows, width), F32),
            jax.ShapeDtypeStruct((items, rows, width), F32),
        ],
        scratch_shapes=[
            pltpu.VMEM((items, rows, width), F32),
            pltpu.VMEM((items, rows, width), F32),
            pltpu.VMEM((width, items * rows), BF16),
            pltpu.VMEM((width, items * rows), BF16),
            pltpu.VMEM((width, hidden), BF16),
            pltpu.VMEM((width, hidden), BF16),
            pltpu.VMEM((hidden, width), BF16),
            pltpu.VMEM((items * rows, 3 * inner), BF16),
            pltpu.VMEM((2, width, 3 * inner), BF16),
            pltpu.VMEM((2, inner, width), BF16),
            pltpu.VMEM((pairs, items, rows, 384), BF16),
            pltpu.VMEM((pairs, items, rows, 2 * rows), BF16),
            pltpu.VMEM((items, inner, rows), BF16),
            pltpu.VMEM((items, inner, rows), BF16),
            pltpu.VMEM((8, width), F32),
            pltpu.SemaphoreType.DMA((13 + 2 * pairs + 8 * items,)),
            pltpu.SemaphoreType.DMA((2, 1 + 2 * pairs)),
        ] + scratch,
        compiler_params=pltpu.CompilerParams(vmem_limit_bytes=(LIMIT if linked else 63) * MIB, **params),
        name="layer",
    )(lengths, group, mask, *gains, *arrays)


def unpack_blocks(width, inner, hidden):
    pairs = HEADS // 2
    blocks = []
    for b in range(hidden // 128):
        blocks.append((8, 0, 128 * b, b, 0, width))
        blocks.append((9, 0, 128 * b, b, width, width))
        for m in range(width // 128):
            blocks.append((10, 128 * b, 128 * m, b, 2 * width + 128 * m, 128))
    base = hidden // 128
    for first_out, start in ((4, base), (0, base + 1 + pairs)):
        for m in range(width // 128):
            blocks.append((first_out + 3, 0, 128 * m, start, inner * m, inner))
        for j in range(pairs):
            for part in range(3):
                blocks.append((first_out + part, 0, 128 * j, start + 1 + j, width * part, width))
    return blocks


def unpack(grads, width, inner, hidden):
    shapes = ([(width, inner)] * 3 + [(inner, width)]) * 2 + [(width, hidden)] * 2 + [(hidden, width)]
    outs = [jnp.zeros(shape, F32) for shape in shapes]
    for out, row, col, unit, start, rows in unpack_blocks(width, inner, hidden):
        outs[out] = outs[out].at[row : row + rows, col : col + 128].set(grads[unit, start : start + rows])
    return outs


def place_kernel(blocks, grads, text_grad, memory_grad, output, gains, counts, *refs):
    outs, (gain_outs, count_out, sem) = refs[:-5], (refs[-5:-2], refs[-2], refs[-1])
    copies = [
        pltpu.make_async_copy(
            grads.at[unit, pl.ds(start, rows), :], outs[3 + out].at[pl.ds(row, rows), pl.ds(col, 128)], sem.at[n]
        )
        for n, (out, row, col, unit, start, rows) in enumerate(blocks)
    ]
    for n, source in enumerate((output, text_grad, memory_grad)):
        copies.append(pltpu.make_async_copy(source, outs[n], sem.at[len(blocks) + n]))
    for copy in copies:
        copy.start()
    for n in range(3):
        gain_outs[n][...] = gains[n]
    for n in range(GROUPS):
        count_out[n] = jnp.sum(counts[0:1, n : n + 1])
    for copy in copies:
        copy.wait()


def place(arrays, width, inner, hidden):
    blocks = unpack_blocks(width, inner, hidden)
    rows = arrays[1].shape
    shapes = ([(width, inner)] * 3 + [(inner, width)]) * 2 + [(width, hidden)] * 2 + [(hidden, width)]
    hbm, vmem = pl.BlockSpec(memory_space=pl.ANY), pl.BlockSpec(memory_space=pltpu.VMEM)
    return pl.pallas_call(
        functools.partial(place_kernel, blocks),
        in_specs=[vmem] * 6,
        out_specs=[hbm] * (3 + len(shapes)) + [vmem] * 3 + [pl.BlockSpec(memory_space=pltpu.SMEM)],
        out_shape=[jax.ShapeDtypeStruct(rows, BF16)] * 3
        + [jax.ShapeDtypeStruct(shape, F32) for shape in shapes]
        + [jax.ShapeDtypeStruct((width,), F32)] * 3
        + [jax.ShapeDtypeStruct((GROUPS,), F32)],
        scratch_shapes=[pltpu.SemaphoreType.DMA((len(blocks) + 3,))],
        compiler_params=pltpu.CompilerParams(vmem_limit_bytes=1 * MIB),
        name="place",
    )(*[pltpu.with_memory_space_constraint(array, pltpu.VMEM) for array in arrays])


def body(
    linked, text_tokens, memory, cotangent, lengths, memory_mask, group_table, self_gain, cross_gain, ffn_gain,
    self_query, self_key, self_value, self_out, cross_query, cross_key, cross_value, cross_out,
    ffn_gate, ffn_up, ffn_down,
):
    items, rows, width = text_tokens.shape
    inner, hidden = self_query.shape[1], ffn_gate.shape[1]
    gains = [gain.reshape(1, width) for gain in (self_gain, cross_gain, ffn_gain)]
    arrays = [
        text_tokens, memory, cotangent, self_query, self_key, self_value, self_out, cross_query, cross_key,
        cross_value, cross_out, ffn_gate, ffn_up, ffn_down,
    ]
    shapes = (items, rows, width, inner, hidden)
    if linked:
        made = run_layer(True, lengths, group_table, memory_mask, gains, arrays, shapes)
        layer_output, text_grad, memory_grad, *outs = place(made[:6], width, inner, hidden)
        return (layer_output, text_grad, memory_grad, *outs[-4:-1], *outs[:-4], outs[-1])
    places = jnp.arange(group_table.shape[0], dtype=jnp.int32)
    own_group = jnp.sum(jnp.where(places == lax.axis_index("wide"), group_table, 0))
    one_hot = (jnp.arange(GROUPS, dtype=jnp.int32) == own_group).astype(F32)
    counts = lax.psum(one_hot * jnp.sum(lengths).astype(F32), AXES)
    root_counts = jnp.sqrt(counts)
    factor = jnp.sum(one_hot * (jnp.sum(counts) / (jnp.sum(root_counts) * root_counts)))
    grads, text_grad, memory_grad, layer_output, gain_grads, *unused = run_layer(
        False, lengths, factor.reshape(1), memory_mask, gains, arrays, shapes
    )
    outs = unpack(lax.psum(factor * grads, AXES), width, inner, hidden)
    gain_grads = lax.psum(factor * gain_grads, AXES)
    return (
        layer_output, text_grad, memory_grad, gain_grads[0], gain_grads[1], gain_grads[2], *outs, counts,
    )


def solution(mesh):
    split, split2, split3, copied = P(AXES), P(AXES, None), P(AXES, None, None), P()
    linked = mesh.shape["wide"] == 8 and mesh.shape["narrow"] == 4
    return jax.shard_map(
        functools.partial(body, linked),
        mesh=mesh,
        in_specs=(split3, split3, split3, split, split2) + (copied,) * 15,
        out_specs=(split3, split3, split3) + (copied,) * 15,
        check_vma=False,
    )
```

```python
import functools

import jax
import jax.numpy as jnp
from jax import lax
from jax.experimental import pallas as pl
from jax.experimental.pallas import tpu as pltpu
from jax.sharding import PartitionSpec as P

HEADS = 6
GROUPS = 2
EPSILON = 1e-06
NEGATIVE = -1e30
F32 = jnp.float32
BF16 = jnp.bfloat16
AXES = ("wide", "narrow")
LIMIT = 44
UNROLL = 4
ROOT = 0.7978845608028654
CUBE = 0.044715
MIB = 1 << 20


def contract(left, right, left_dim, right_dim):
    return lax.dot_general(
        left, right, (((left_dim,), (right_dim,)), ((), ())), preferred_element_type=F32
    )


def nn(left, right):
    return contract(left, right, 1, 0)


def nt(left, right):
    return contract(left, right, 1, 1)


def tn(left, right):
    return contract(left, right, 0, 0)


def norm_scale(values):
    return lax.rsqrt(jnp.mean(values * values, axis=-1, keepdims=True) + EPSILON)


def norm_back(values, gain, grad):
    scale = norm_scale(values)
    unit = values * scale
    gain_rows = grad * unit
    dot = jnp.mean(gain_rows * gain, axis=-1, keepdims=True)
    return scale * (grad * gain - unit * dot), jnp.sum(gain_rows, axis=0, keepdims=True)


def low_lanes(rows):
    return lax.broadcasted_iota(jnp.int32, (rows, 128), 1) < 64


def stack_heads(pair, low):
    zero = jnp.zeros_like(pair)
    return jnp.concatenate([jnp.where(low, pair, zero), jnp.where(low, zero, pair)], axis=0)


def spread_heads(turned):
    zero = jnp.zeros_like(turned[:64])
    return jnp.concatenate(
        [jnp.concatenate([turned[:64], zero], axis=0), jnp.concatenate([zero, turned[64:]], axis=0)], axis=1
    )


def join_heads(turned):
    count = turned.shape[1] // 2
    return jnp.concatenate([turned[:64, :count], turned[64:, count:]], axis=0)


def pair_slice(values, index):
    return values[:, 128 * index : 128 * index + 128]


RISE = (0, 1, 3, 5, 7, 9, 10, 12, 14, 15)
HALVES = 5
LEGS = 2 * HALVES - 1


def exchange_plan():
    wide, narrow = lax.axis_index("wide"), lax.axis_index("narrow")
    z, y = wide // 2, wide % 2
    x, core = narrow // 2, narrow % 2
    near, far = z % 2, z // 2
    flip_x = (wide, (1 - x) * 2 + core)
    flip_y = (z * 2 + 1 - y, narrow)
    flip_core = (wide, x * 2 + 1 - core)
    flip_near = ((far * 2 + 1 - near) * 2 + y, narrow)
    flip_far = (((1 - far) * 2 + near) * 2 + y, narrow)

    def choose(first, second):
        return first + core * (second - first)

    first_flip = tuple(choose(a, b) for a, b in zip(flip_x, flip_y))
    third_flip = tuple(choose(b, a) for a, b in zip(flip_x, flip_y))
    bits = (core, choose(x, y), near, choose(y, x), far)
    partners = (flip_core, first_flip, flip_near, third_flip, flip_far)
    plain = (flip_core, flip_x, flip_near, flip_y, flip_far)
    return bits, partners, plain


def attend(query, key, value, mask, keep):
    low = low_lanes(query.shape[0])
    query = (query * 0.125).astype(BF16)
    key = key.astype(BF16)
    value = value.astype(BF16)
    mixed = []
    for j in range(HEADS // 2):
        q, k, v = pair_slice(query, j), pair_slice(key, j), pair_slice(value, j)
        scores = mask(nt(k, stack_heads(q, low)))
        top = jnp.max(scores, axis=0, keepdims=True)
        expo = jnp.exp(scores - top)
        total = jnp.sum(expo, axis=0, keepdims=True)
        prob = (expo * (1.0 / total)).astype(BF16)
        mixed.append(join_heads(nn(v.T, prob)))
        keep(j, q, k, v, prob)
    return jnp.concatenate(mixed, axis=0).astype(BF16)


def layer_kernel(
    linked, items, rows, width, inner, hidden,
    len_ref, group_ref, mask_ref, self_gain, cross_gain, ffn_gain,
    text_hbm, mem_hbm, cot_hbm, sq_hbm, sk_hbm, sv_hbm, so_hbm, cq_hbm, ck_hbm, cv_hbm, co_hbm,
    gate_hbm, up_hbm, down_hbm,
    grads, first, second, output, gain_out, counts_ref,
    sqkv_hbm, sprob_hbm, smix_hbm, mid_hbm, post_hbm,
    *rest,
):
    (xf, din, first_t, second_t, gate, up, down, work, wqkv, wout, qkv, prob, mix, dmix, gain_grads,
     load_sem, save_sem) = rest[:17]
    if linked:
        halves, small, small_in, factor_ref, send_sem, recv_sem, small_send, small_recv, free_sem = rest[17:]
    pairs = HEADS // 2
    chunk = 256
    chunks = hidden // chunk
    low = low_lanes(rows)
    units = 2 * chunks + 2 * (1 + pairs)
    last_tick = 2 * (units - 1) + RISE[-1]
    if linked:
        bits, partners, plain = exchange_plan()
        barrier = pltpu.get_barrier_semaphore()
        for device in (plain[0], plain[1], plain[2], plain[3], plain[4]):
            pl.semaphore_signal(barrier, inc=1, device_id=device, device_id_type=pl.DeviceIdType.MESH)
        pl.semaphore_wait(barrier, len(plain))

    half = 3 * width // 2

    def region(step, own):
        start = 0
        for s in range(step + 1):
            bit = bits[s] if own or s < step else 1 - bits[s]
            start = start + bit * (half >> s)
        return pl.ds(pl.multiple_of(start, 16), half >> step)

    def half_rows(step):
        size = half >> min(step, HALVES - 2)
        return pl.ds(2 * half - (2 * half >> step), size)

    def stage_copy(index, k):
        slot = k % 2 if isinstance(k, int) else lax.rem(k, 2)
        if index < HALVES:
            sent = region(index, False) if index < HALVES - 1 else region(HALVES - 2, True)
            source, target = grads.at[k, sent], halves.at[slot, half_rows(index)]
            step = index
        else:
            step = LEGS - 1 - index
            source = target = grads.at[k, region(step, True)]
        return pltpu.make_async_remote_copy(
            src_ref=source, dst_ref=target, send_sem=send_sem.at[slot, index], recv_sem=recv_sem.at[slot, index],
            device_id=partners[step], device_id_type=pl.DeviceIdType.MESH,
        )

    def advance(index, k):
        slot = k % 2 if isinstance(k, int) else lax.rem(k, 2)
        if index > 0:
            stage_copy(index - 1, k).wait()
        if 0 < index <= HALVES:
            step = min(index - 1, HALVES - 2)
            own = region(step, True)
            value = grads[k, own, :] + halves[slot, half_rows(index - 1), :]
            if index == 1:
                value = value * factor_ref[0:1, :]
            grads[k, own, :] = value
            if index < HALVES:
                pl.semaphore_signal(
                    free_sem.at[k, step], inc=1, device_id=partners[step], device_id_type=pl.DeviceIdType.MESH
                )
        if index < LEGS:
            if index >= HALVES:
                pl.semaphore_wait(free_sem.at[k, LEGS - 1 - index], 1)
            stage_copy(index, k).start()

    def tick(t):
        if not linked:
            return
        for index in reversed(range(LEGS + 1)):
            u = t - RISE[index]
            if isinstance(t, int):
                if u >= 0 and u % 2 == 0 and u < 2 * units:
                    advance(index, u // 2)
            else:
                ready = (u >= 0) & (u < 2 * units) & (lax.rem(u + 32, 2) == 0)
                pl.when(ready)(functools.partial(advance, index, u // 2))

    def small_copy(use, step):
        return pltpu.make_async_remote_copy(
            src_ref=small.at[use, step], dst_ref=small_in.at[use, step],
            send_sem=small_send.at[use, step], recv_sem=small_recv.at[use, step],
            device_id=plain[step], device_id_type=pl.DeviceIdType.MESH,
        )

    def small_step(use, step):
        if not linked:
            return
        if step > 0:
            small_copy(use, step - 1).wait()
            small[use, step] = small[use, step - 1] + small_in[use, step - 1]
        if step < HALVES:
            small_copy(use, step).start()

    if linked:
        total = len_ref[0]
        for i in range(1, items):
            total = total + len_ref[i]
        lane = lax.broadcasted_iota(jnp.int32, (8, width), 1)
        small[0, 0] = jnp.where(lane == group_ref[lax.axis_index("wide")], total.astype(F32), 0.0)
        small_step(0, 0)

    def set_factor():
        if not linked:
            return
        counts = small[0, HALVES]
        lane = lax.broadcasted_iota(jnp.int32, (8, width), 1)
        counts_ref[...] = counts[:, 0:128]
        roots = jnp.sqrt(counts)
        own = jnp.sum(jnp.where(lane == group_ref[lax.axis_index("wide")], roots, 0.0), axis=-1, keepdims=True)
        top = jnp.sum(counts, axis=-1, keepdims=True)
        bottom = jnp.sum(roots, axis=-1, keepdims=True) * own
        factor_ref[...] = jnp.broadcast_to(top / bottom, (8, 128))

    def scaled(values):
        if linked:
            return values * factor_ref[0:1, 0:1]
        return values * group_ref[0]

    def item_rows(i):
        return pl.ds(pl.multiple_of(i * rows, rows), rows)

    def each_item(body, *marks):
        several(items, body, *marks)

    def several(count, body, *marks):
        def step(i, carry):
            body(i)
            for place, time in marks:
                pl.when(i == place)(functools.partial(tick, time))
            return carry

        lax.fori_loop(0, count, step, 0)

    def load(index, source, target):
        return pltpu.make_async_copy(source, target, load_sem.at[index])

    def weights(base, which, query, key, value, out):
        return [
            load(base, query, wqkv.at[which, :, pl.ds(0, inner)]),
            load(base + 1, key, wqkv.at[which, :, pl.ds(inner, inner)]),
            load(base + 2, value, wqkv.at[which, :, pl.ds(2 * inner, inner)]),
            load(base + 3, out, wout.at[which]),
        ]

    middle = items // 2 - 1
    final = items - 1
    self_weights = weights(0, 1, sq_hbm, sk_hbm, sv_hbm, so_hbm)
    cross_weights = weights(4, 0, cq_hbm, ck_hbm, cv_hbm, co_hbm)
    ffn_loads = [load(8, gate_hbm, gate), load(9, up_hbm, up), load(10, down_hbm, down)]
    text_again = load(11, text_hbm, first)
    smix_load = load(12, smix_hbm, mix)

    def pair_loads(j):
        return [load(13 + j, sqkv_hbm.at[j], qkv.at[j]), load(13 + pairs + j, sprob_hbm.at[j], prob.at[j])]

    lists = 13 + 2 * pairs

    def text_load(i):
        return load(lists + i, text_hbm.at[i], first.at[i])

    def mem_load(i):
        return load(lists + items + i, mem_hbm.at[i], second.at[i])

    def cot_load(i):
        return load(lists + 2 * items + i, cot_hbm.at[i], second.at[i])

    def mem_again(i):
        return load(lists + 3 * items + i, mem_hbm.at[i], work.at[item_rows(i), pl.ds(0, width)])

    def mid_save(i):
        return load(lists + 4 * items + i, din.at[i], mid_hbm.at[i])

    def post_save(i):
        return load(lists + 5 * items + i, xf.at[i], post_hbm.at[i])

    def post_load(i):
        return load(lists + 6 * items + i, post_hbm.at[i], xf.at[i])

    def mid_load(i):
        return load(lists + 7 * items + i, mid_hbm.at[i], xf.at[i])

    for copy in self_weights:
        copy.start()
    for i in range(items):
        text_load(i).start()
    for copy in cross_weights:
        copy.start()
    for i in range(items):
        mem_load(i).start()
    for copy in ffn_loads:
        copy.start()
    gain_grads[...] = jnp.zeros_like(gain_grads)

    def prob_stage(u, j):
        return work.at[pl.ds(rows * (pairs * u + j), rows), pl.ds(0, 2 * rows)]

    def qkv_stage(u, j):
        return work.at[pl.ds(rows * (pairs * u + j), rows), pl.ds(2 * rows, 384)]

    def mix_stage(u):
        return work.at[pl.ds(2 * rows * pairs, inner), pl.ds(rows * u, rows)]

    def saves(u, i):
        copies = [pltpu.make_async_copy(mix_stage(u), smix_hbm.at[i], save_sem.at[u, 0])]
        for j in range(pairs):
            copies.append(pltpu.make_async_copy(qkv_stage(u, j), sqkv_hbm.at[j, i], save_sem.at[u, 1 + j]))
            copies.append(pltpu.make_async_copy(prob_stage(u, j), sprob_hbm.at[j, i], save_sem.at[u, 1 + pairs + j]))
        return copies

    for copy in self_weights:
        copy.wait()
    row = lax.broadcasted_iota(jnp.int32, (rows, 2 * rows), 0)
    col = lax.broadcasted_iota(jnp.int32, (rows, 2 * rows), 1)
    causal = row <= jnp.where(col >= rows, col - rows, col)
    turned_mask = mask_ref[...].astype(F32).T
    item_lane = lax.broadcasted_iota(jnp.int32, (rows, items), 1)

    def forward_two(b, carry):
        numbers = (2 * b, 2 * b + 1)

        @pl.when(b > 0)
        def _():
            for u in range(2):
                for copy in saves(u, 2 * b - 2 + u):
                    copy.wait()

        for i in numbers:
            text_load(i).wait()
        text = first[pl.ds(2 * b, 2)].reshape(2 * rows, width).astype(F32)
        self_in = (text * norm_scale(text) * self_gain[...]).astype(BF16)
        proj = nn(self_in, wqkv[1])
        mixed = []
        for u, i in enumerate(numbers):
            allowed = causal & (row < len_ref[i])
            mine = proj[u * rows : u * rows + rows]

            def keep(j, q, k, v, chance):
                qkv_stage(u, j)[:, 0:128] = q
                qkv_stage(u, j)[:, 128:256] = k
                qkv_stage(u, j)[:, 256:384] = v
                prob_stage(u, j)[...] = chance

            mixed.append(
                attend(
                    mine[:, :inner], mine[:, inner : 2 * inner], mine[:, 2 * inner :],
                    lambda s: jnp.where(allowed, s, NEGATIVE), keep,
                )
            )
            mix_stage(u)[...] = mixed[u]
            for copy in saves(u, i):
                copy.start()

        @pl.when(b == 0)
        def _():
            for copy in cross_weights:
                copy.wait()

        mid = text + tn(jnp.concatenate(mixed, axis=1), wout[1])
        din[pl.ds(2 * b, 2)] = mid.reshape(2, rows, width)
        for i in numbers:
            mid_save(i).start()
        cross_in = (mid * norm_scale(mid) * cross_gain[...]).astype(BF16)
        output[pl.ds(2 * b, 2)] = cross_in.reshape(2, rows, width)
        query = nn(cross_in, wqkv[0, :, 0:inner])
        for i in numbers:
            mem_load(i).wait()
        proj = nn(second[pl.ds(2 * b, 2)].reshape(2 * rows, width), wqkv[0, :, inner : 3 * inner])
        mixed = []
        for u, i in enumerate(numbers):
            cot_load(i).start()
            open_keys = jnp.sum(jnp.where(item_lane == i, turned_mask, 0.0), axis=-1, keepdims=True) > 0.0
            mine = proj[u * rows : u * rows + rows]

            def keep(j, q, k, v, chance):
                qkv[j, i, :, 0:128] = q
                qkv[j, i, :, 128:256] = k
                qkv[j, i, :, 256:384] = v
                prob[j, i] = chance

            mixed.append(
                attend(
                    query[u * rows : u * rows + rows], mine[:, :inner], mine[:, inner:],
                    lambda s: jnp.where(open_keys, s, NEGATIVE), keep,
                )
            )
            mix[i] = mixed[u]
        post = mid + tn(jnp.concatenate(mixed, axis=1), wout[0])
        xf[pl.ds(2 * b, 2)] = post.reshape(2, rows, width)
        for i in numbers:
            post_save(i).start()
        ffn_in = (post * norm_scale(post) * ffn_gain[...]).astype(BF16)
        first[pl.ds(2 * b, 2)] = ffn_in.reshape(2, rows, width)
        first_t[:, pl.ds(pl.multiple_of(2 * b * rows, 2 * rows), 2 * rows)] = ffn_in.T
        for s in range(1, HALVES):
            pl.when(b == s - 1)(functools.partial(small_step, 0, s))
        return carry

    lax.fori_loop(0, items // 2, forward_two, 0)
    for u in range(2):
        for copy in saves(u, items - 2 + u):
            copy.wait()

    def prepare(i):
        cot_load(i).wait()
        row = lax.broadcasted_iota(jnp.int32, (rows, width), 0)
        masked = jnp.where(row < len_ref[i], second[i], jnp.zeros((), BF16))
        second[i] = masked
        second_t[:, item_rows(i)] = masked.T
        mid_save(i).wait()
        post_save(i).wait()

    each_item(prepare)
    for copy in ffn_loads:
        copy.wait()
    small_step(0, HALVES)
    set_factor()

    def ffn_parts(c):
        cols = pl.ds(pl.multiple_of(c * chunk, chunk), chunk)
        return gate.at[:, cols], up.at[:, cols], down.at[cols, :]

    def ffn_grads(c):
        both = nn(first_t[...], work[:, 0 : 2 * chunk])
        turned = nn(second_t[...], work[:, 2 * chunk : 3 * chunk])
        for h in range(chunk // 128):
            place = (chunk // 128) * c + h
            grads[place, 0:width, :] = pair_slice(both, h)
            grads[place, width : 2 * width, :] = pair_slice(both, chunk // 128 + h)
            for m in range(width // 128):
                grads[place, 2 * width + 128 * m : 2 * width + 128 * m + 128, :] = (
                    turned[128 * m : 128 * m + 128, 128 * h : 128 * h + 128].T
                )

    def ffn_front(c):
        wg, wu, wd = ffn_parts(c)

        def elementwise(i):
            source = first[i]
            g = nn(source, wg[...])
            u = nn(source, wu[...])
            dh = nt(second[i], wd[...])
            square = g * g
            t = jnp.tanh(g * (ROOT + (ROOT * CUBE) * square))
            cdf = 0.5 + 0.5 * t
            act = g * cdf
            slope = cdf + 0.5 * g * (1.0 - t * t) * (ROOT + (3.0 * ROOT * CUBE) * square)
            work[item_rows(i), 0:chunk] = (dh * u * slope).astype(BF16)
            work[item_rows(i), chunk : 2 * chunk] = (dh * act).astype(BF16)
            work[item_rows(i), 2 * chunk : 3 * chunk] = (act * u).astype(BF16)

        each_item(elementwise, (middle, 4 * c - 1))
        ffn_grads(c)
        tick(4 * c)

    def back_part(c, i):
        wg, wu, wd = ffn_parts(c)
        return nt(work[item_rows(i), 0:chunk], wg[...]) + nt(work[item_rows(i), chunk : 2 * chunk], wu[...])

    def out_part(c, i):
        wg, wu, wd = ffn_parts(c)
        return xf[i] + nn(work[item_rows(i), 2 * chunk : 3 * chunk], wd[...])

    def ffn_chunk(c, carry):
        ffn_front(c)

        def spread(i):
            xf[i] = out_part(c, i)
            din[i] = jnp.where(c == 0, 0.0, din[i]) + back_part(c, i)

        each_item(spread, (middle, 4 * c + 1), (final, 4 * c + 2))
        return carry

    lax.fori_loop(0, chunks - 1, ffn_chunk, 0)
    ffn_front(chunks - 1)
    text_again.start()
    clock = 4 * (chunks - 1)

    def spread_last(i):
        din[i] += back_part(chunks - 1, i)
        done = out_part(chunks - 1, i).astype(BF16)
        first_t[:, item_rows(i)] = output[i].T
        output[i] = done
        post_load(i).start()
        mem_again(i).start()

    each_item(spread_last, (middle, clock + 1), (final, clock + 2))
    clock += 2

    def two(b):
        return pl.ds(2 * b, 2)

    def two_rows(b):
        return pl.ds(pl.multiple_of(2 * b * rows, 2 * rows), 2 * rows)

    def flat(values):
        return values.reshape(2 * rows, width)

    def send_back(place, b, total, which):
        din[two(b)] = total.reshape(2, rows, width)
        branch = total.astype(BF16)
        turned = nt(wout[which], branch).astype(BF16)
        dmix[2 * b] = turned[:, :rows]
        dmix[2 * b + 1] = turned[:, rows:]
        product = nn(mix[2 * b], branch[:rows]) + nn(mix[2 * b + 1], branch[rows:])
        for m in range(width // 128):
            grads[place, inner * m : inner * m + inner, :] += pair_slice(product, m)

    base = 2 * chunks
    grads[base] = jnp.zeros((3 * width, 128), F32)

    def cross_start(b):
        for u in range(2):
            post_load(2 * b + u).wait()
        back, gain_rows = norm_back(flat(xf[two(b)]), ffn_gain[...], flat(din[two(b)]))
        for u in range(2):
            mid_load(2 * b + u).start()
        gain_grads[2:3] += gain_rows
        send_back(base, b, flat(second[two(b)]).astype(F32) + back, 0)
        for u in range(2):
            mem_again(2 * b + u).wait()
        second_t[:, two_rows(b)] = work[two_rows(b), 0:width].T

    several(items // 2, cross_start, (items // 4 - 1, clock + 1), (items // 2 - 1, clock + 2))
    clock += 2

    def pair_terms(j, i):
        lanes = pl.ds(pl.multiple_of(j * 128, 128), 128)
        q, k, v = qkv[j, i, :, 0:128], qkv[j, i, :, 128:256], qkv[j, i, :, 256:384]
        return q, k, v, prob[j, i], dmix[i, lanes, :], mix[i, lanes, :]

    def pair_math(q, k, v, chance, grad, mixed):
        product = grad.astype(F32) * mixed.astype(F32)
        sums = jnp.concatenate(
            [jnp.sum(product[:64], axis=0, keepdims=True), jnp.sum(product[64:], axis=0, keepdims=True)], axis=1
        )
        grad2 = spread_heads(grad)
        score_grad = (chance.astype(F32) * (nn(v, grad2) - sums)).astype(BF16)
        dq = join_heads(nn(k.T, score_grad)) * 0.125
        dk = nn(score_grad, stack_heads(q, low))
        dv = nt(chance, grad2)
        return dq.astype(BF16).T, dk.astype(BF16), dv.astype(BF16)

    def pair_back(j, b):
        numbers = [UNROLL * b + u for u in range(UNROLL)]
        terms = [pair_terms(j, i) for i in numbers]
        made = [pair_math(*entry) for entry in terms]
        for i, entry in zip(numbers, made):
            for part in range(3):
                lanes = pl.ds(pl.multiple_of(part * inner + j * 128, 128), 128)
                work[item_rows(i), lanes] = entry[part]

    def pair_grads(place, j, inputs):
        for part in range(3):
            lanes = pl.ds(pl.multiple_of(part * inner + j * 128, 128), 128)
            grads[place, width * part : width * part + width, :] = nn(inputs[part][...], work[:, lanes])

    def cross_pair(j, carry):
        several(items // UNROLL, functools.partial(pair_back, j), (items // UNROLL // 2 - 1, clock + 1 + 2 * j))
        pair_grads(base + 1 + j, j, (first_t, second_t, second_t))
        for copy in pair_loads(j):
            copy.start()
        tick(clock + 2 + 2 * j)
        return carry

    lax.fori_loop(0, pairs, cross_pair, 0)
    clock += 2 * pairs
    smix_load.start()
    text_again.wait()
    smix_load.wait()
    grads[base + 1 + pairs] = jnp.zeros((3 * width, 128), F32)

    def self_start(b):
        dcross = nt(work[two_rows(b), 0:inner], wqkv[0, :, 0:inner])
        dmem = nt(work[two_rows(b), inner : 3 * inner], wqkv[0, :, inner : 3 * inner])
        second[two(b)] = scaled(dmem).astype(BF16).reshape(2, rows, width)
        for u in range(2):
            mid_load(2 * b + u).wait()
        back, gain_rows = norm_back(flat(xf[two(b)]), cross_gain[...], dcross)
        gain_grads[1:2] += gain_rows
        send_back(base + 1 + pairs, b, flat(din[two(b)]) + back, 1)
        text = flat(first[two(b)]).astype(F32)
        self_in = (text * norm_scale(text) * self_gain[...]).astype(BF16)
        first_t[:, two_rows(b)] = self_in.T

    several(items // 2, self_start, (items // 4 - 1, clock + 1), (items // 2 - 1, clock + 2))
    clock += 2

    def self_pair(j, carry):
        for copy in pair_loads(j):
            copy.wait()
        several(items // UNROLL, functools.partial(pair_back, j), (items // UNROLL // 2 - 1, clock + 1 + 2 * j))
        pair_grads(base + 2 + pairs + j, j, (first_t, first_t, first_t))
        tick(clock + 2 + 2 * j)
        return carry

    lax.fori_loop(0, pairs, self_pair, 0)
    clock += 2 * pairs

    def finish(b):
        dself = nt(work[two_rows(b), :], wqkv[1])
        back, gain_rows = norm_back(flat(first[two(b)]).astype(F32), self_gain[...], dself)
        gain_grads[0:1] += gain_rows
        made = scaled(flat(din[two(b)]) + back).astype(BF16)
        first[two(b)] = made.reshape(2, rows, width)

    several(items // 2, finish, (items // 4 - 1, clock + 1), (items // 2 - 1, clock + 2))
    clock += 2
    if linked:
        small[1, 0] = scaled(gain_grads[...])
        small_step(1, 0)
        for step in range(1, max(last_tick - clock, HALVES) + 1):
            if clock + step <= last_tick:
                tick(clock + step)
            if step <= HALVES:
                small_step(1, step)
        gain_out[...] = small[1, HALVES]
    else:
        gain_out[...] = gain_grads[...]
        counts_ref[...] = jnp.zeros_like(counts_ref)


def run_layer(linked, lengths, group, mask, gains, arrays, shapes):
    items, rows, width, inner, hidden = shapes
    pairs = HEADS // 2
    units = 2 * (hidden // 256) + 2 * (1 + pairs)
    hbm = pl.BlockSpec(memory_space=pl.ANY)
    vmem = pl.BlockSpec(memory_space=pltpu.VMEM)
    smem = pl.BlockSpec(memory_space=pltpu.SMEM)
    place_in = pltpu.VMEM if linked else jax.ShapeDtypeStruct
    scratch, params = [], {}
    if linked:
        scratch = [
            pltpu.VMEM((2, 3 * width, 128), F32),
            pltpu.VMEM((2, HALVES + 1, 8, width), F32),
            pltpu.VMEM((2, HALVES, 8, width), F32),
            pltpu.VMEM((8, 128), F32),
            pltpu.SemaphoreType.DMA((2, LEGS)),
            pltpu.SemaphoreType.DMA((2, LEGS)),
            pltpu.SemaphoreType.DMA((2, HALVES)),
            pltpu.SemaphoreType.DMA((2, HALVES)),
            pltpu.SemaphoreType.REGULAR((units, HALVES - 1)),
        ]
        params = dict(collective_id=0, has_side_effects=True)
    return pl.pallas_call(
        functools.partial(layer_kernel, linked, items, rows, width, inner, hidden),
        in_specs=[smem, smem, vmem, vmem, vmem, vmem] + [hbm] * len(arrays),
        out_specs=[vmem] * 6 + [hbm] * 5,
        out_shape=[
            place_in((units, 3 * width, 128), F32),
            place_in((items, rows, width), BF16),
            place_in((items, rows, width), BF16),
            place_in((items, rows, width), BF16),
            place_in((8, width), F32),
            place_in((8, 128), F32),
            jax.ShapeDtypeStruct((pairs, items, rows, 384), BF16),
            jax.ShapeDtypeStruct((pairs, items, rows, 2 * rows), BF16),
            jax.ShapeDtypeStruct((items, inner, rows), BF16),
            jax.ShapeDtypeStruct((items, rows, width), F32),
            jax.ShapeDtypeStruct((items, rows, width), F32),
        ],
        scratch_shapes=[
            pltpu.VMEM((items, rows, width), F32),
            pltpu.VMEM((items, rows, width), F32),
            pltpu.VMEM((width, items * rows), BF16),
            pltpu.VMEM((width, items * rows), BF16),
            pltpu.VMEM((width, hidden), BF16),
            pltpu.VMEM((width, hidden), BF16),
            pltpu.VMEM((hidden, width), BF16),
            pltpu.VMEM((items * rows, 3 * inner), BF16),
            pltpu.VMEM((2, width, 3 * inner), BF16),
            pltpu.VMEM((2, inner, width), BF16),
            pltpu.VMEM((pairs, items, rows, 384), BF16),
            pltpu.VMEM((pairs, items, rows, 2 * rows), BF16),
            pltpu.VMEM((items, inner, rows), BF16),
            pltpu.VMEM((items, inner, rows), BF16),
            pltpu.VMEM((8, width), F32),
            pltpu.SemaphoreType.DMA((13 + 2 * pairs + 8 * items,)),
            pltpu.SemaphoreType.DMA((2, 1 + 2 * pairs)),
        ] + scratch,
        compiler_params=pltpu.CompilerParams(vmem_limit_bytes=(LIMIT if linked else 63) * MIB, **params),
        name="layer",
    )(lengths, group, mask, *gains, *arrays)


def unpack_blocks(width, inner, hidden):
    pairs = HEADS // 2
    blocks = []
    for b in range(hidden // 128):
        blocks.append((8, 0, 128 * b, b, 0, width))
        blocks.append((9, 0, 128 * b, b, width, width))
        for m in range(width // 128):
            blocks.append((10, 128 * b, 128 * m, b, 2 * width + 128 * m, 128))
    base = hidden // 128
    for first_out, start in ((4, base), (0, base + 1 + pairs)):
        for m in range(width // 128):
            blocks.append((first_out + 3, 0, 128 * m, start, inner * m, inner))
        for j in range(pairs):
            for part in range(3):
                blocks.append((first_out + part, 0, 128 * j, start + 1 + j, width * part, width))
    return blocks


def unpack(grads, width, inner, hidden):
    shapes = ([(width, inner)] * 3 + [(inner, width)]) * 2 + [(width, hidden)] * 2 + [(hidden, width)]
    outs = [jnp.zeros(shape, F32) for shape in shapes]
    for out, row, col, unit, start, rows in unpack_blocks(width, inner, hidden):
        outs[out] = outs[out].at[row : row + rows, col : col + 128].set(grads[unit, start : start + rows])
    return outs


def place_kernel(blocks, grads, text_grad, memory_grad, output, gains, counts, *refs):
    outs, (gain_outs, count_out, sem) = refs[:-5], (refs[-5:-2], refs[-2], refs[-1])
    copies = [
        pltpu.make_async_copy(
            grads.at[unit, pl.ds(start, rows), :], outs[3 + out].at[pl.ds(row, rows), pl.ds(col, 128)], sem.at[n]
        )
        for n, (out, row, col, unit, start, rows) in enumerate(blocks)
    ]
    for n, source in enumerate((output, text_grad, memory_grad)):
        copies.append(pltpu.make_async_copy(source, outs[n], sem.at[len(blocks) + n]))
    for copy in copies:
        copy.start()
    for n in range(3):
        gain_outs[n][...] = gains[n]
    for n in range(GROUPS):
        count_out[n] = jnp.sum(counts[0:1, n : n + 1])
    for copy in copies:
        copy.wait()


def place(arrays, width, inner, hidden):
    blocks = unpack_blocks(width, inner, hidden)
    rows = arrays[1].shape
    shapes = ([(width, inner)] * 3 + [(inner, width)]) * 2 + [(width, hidden)] * 2 + [(hidden, width)]
    hbm, vmem = pl.BlockSpec(memory_space=pl.ANY), pl.BlockSpec(memory_space=pltpu.VMEM)
    return pl.pallas_call(
        functools.partial(place_kernel, blocks),
        in_specs=[vmem] * 6,
        out_specs=[hbm] * (3 + len(shapes)) + [vmem] * 3 + [pl.BlockSpec(memory_space=pltpu.SMEM)],
        out_shape=[jax.ShapeDtypeStruct(rows, BF16)] * 3
        + [jax.ShapeDtypeStruct(shape, F32) for shape in shapes]
        + [jax.ShapeDtypeStruct((width,), F32)] * 3
        + [jax.ShapeDtypeStruct((GROUPS,), F32)],
        scratch_shapes=[pltpu.SemaphoreType.DMA((len(blocks) + 3,))],
        compiler_params=pltpu.CompilerParams(vmem_limit_bytes=1 * MIB),
        name="place",
    )(*[pltpu.with_memory_space_constraint(array, pltpu.VMEM) for array in arrays])


def body(
    linked, text_tokens, memory, cotangent, lengths, memory_mask, group_table, self_gain, cross_gain, ffn_gain,
    self_query, self_key, self_value, self_out, cross_query, cross_key, cross_value, cross_out,
    ffn_gate, ffn_up, ffn_down,
):
    items, rows, width = text_tokens.shape
    inner, hidden = self_query.shape[1], ffn_gate.shape[1]
    gains = [gain.reshape(1, width) for gain in (self_gain, cross_gain, ffn_gain)]
    arrays = [
        text_tokens, memory, cotangent, self_query, self_key, self_value, self_out, cross_query, cross_key,
        cross_value, cross_out, ffn_gate, ffn_up, ffn_down,
    ]
    shapes = (items, rows, width, inner, hidden)
    if linked:
        made = run_layer(True, lengths, group_table, memory_mask, gains, arrays, shapes)
        layer_output, text_grad, memory_grad, *outs = place(made[:6], width, inner, hidden)
        return (layer_output, text_grad, memory_grad, *outs[-4:-1], *outs[:-4], outs[-1])
    places = jnp.arange(group_table.shape[0], dtype=jnp.int32)
    own_group = jnp.sum(jnp.where(places == lax.axis_index("wide"), group_table, 0))
    one_hot = (jnp.arange(GROUPS, dtype=jnp.int32) == own_group).astype(F32)
    counts = lax.psum(one_hot * jnp.sum(lengths).astype(F32), AXES)
    root_counts = jnp.sqrt(counts)
    factor = jnp.sum(one_hot * (jnp.sum(counts) / (jnp.sum(root_counts) * root_counts)))
    grads, text_grad, memory_grad, layer_output, gain_grads, *unused = run_layer(
        False, lengths, factor.reshape(1), memory_mask, gains, arrays, shapes
    )
    outs = unpack(lax.psum(factor * grads, AXES), width, inner, hidden)
    gain_grads = lax.psum(factor * gain_grads, AXES)
    return (
        layer_output, text_grad, memory_grad, gain_grads[0], gain_grads[1], gain_grads[2], *outs, counts,
    )


def solution(mesh):
    split, split2, split3, copied = P(AXES), P(AXES, None), P(AXES, None, None), P()
    linked = mesh.shape["wide"] == 8 and mesh.shape["narrow"] == 4
    return jax.shard_map(
        functools.partial(body, linked),
        mesh=mesh,
        in_specs=(split3, split3, split3, split, split2) + (copied,) * 15,
        out_specs=(split3, split3, split3) + (copied,) * 15,
        check_vma=False,
    )
```
